256 devices in a mesh: fsdp: 8 (over y_lo, x), sp: 32 (over y_hi, z, core).
Axes of the slice: x: 4, y: 4 (y_hi: 2, y_lo: 2; y = y_hi * 2 + y_lo), z: 8, core: 2. Of those that a mesh axis runs over, the one named last changes fastest.
Arguments:
- queries: bfloat16 [24576, 3072], P('sp', 'fsdp'), may hold values from -6 to 6
- keys: bfloat16 [24576, 3072], P('sp', 'fsdp'), may hold values from -6 to 6
- values: bfloat16 [24576, 3072], P('sp', 'fsdp'), may hold values from -6 to 6
- w_out: bfloat16 [3072, 3072], P('fsdp', 'sp'), may hold values from -0.109375 to 0.109375
- grad_out: bfloat16 [24576, 3072], P('sp', 'fsdp'), may hold values from -6 to 6
- neighbors: int32 [64, 5], P('sp'), may hold values from -1 to 63, as said below
Outputs:
- output: bfloat16 [24576, 3072], P('sp', 'fsdp')
- grad_queries: bfloat16 [24576, 3072], P('sp', 'fsdp')
- grad_keys: bfloat16 [24576, 3072], P('sp', 'fsdp')
- grad_values: bfloat16 [24576, 3072], P('sp', 'fsdp')
- grad_weight: float32 [3072, 3072], P('fsdp', 'sp')
The draws below stay inside these ranges and needn't reach their ends.
Inputs may be any that keep to these rules, and one draw needn't show every extreme that they name: `neighbors`: row t lists first, in ascending order, the distinct tiles that the queries of tile t attend to, each within 2 tiles of t and t itself always among them, then -1 in the unused slots; some row fills all 5 slots. Where they exist, tile t - 1 is listed for every t that is a multiple of 2, and tile t + 1 for every t one less than a multiple of 2.
All inputs are finite; a program needn't handle non-finite values.
Results may differ from the reference program's by a relative error of at most 0.02.
Values may be sent and summed in bfloat16 or wider, within the bound.
A program may use at most 128 MiB of HBM per device.

```python
import math
import jax
import jax.numpy as jnp
from jax import lax

D = 3072
H = 24
HD = 128
TILE = 384
REACH = 2
TILES_DEV = 2
NB = 5
TILES = 64
TOKENS = 24576


def draw_queries(key, part):
    key = jax.random.fold_in(key, 1)
    base_values = jnp.clip(jax.random.normal(key, (TOKENS, D), jnp.float32), -6.0, 6.0)
    return base_values.astype(jnp.bfloat16)


def draw_keys(key, part):
    key = jax.random.fold_in(key, 2)
    base_values = jnp.clip(jax.random.normal(key, (TOKENS, D), jnp.float32), -6.0, 6.0)
    return base_values.astype(jnp.bfloat16)


def draw_neighbors(key, part):
    key = jax.random.fold_in(key, 7)
    offsets = jnp.arange(-REACH, REACH + 1, dtype=jnp.int32)
    tile_ids = jnp.arange(TILES, dtype=jnp.int32)[:, None]
    local_pos = tile_ids % TILES_DEV
    candidates = tile_ids + offsets[None, :]
    random_bits = jax.random.randint(key, (TILES, NB), 0, 4)
    thresholds = jnp.maximum(4 - jnp.abs(offsets), 1)
    keep_slot = (random_bits < thresholds[None, :]) | (offsets[None, :] == 0) | (tile_ids == REACH)
    keep_slot = keep_slot | (local_pos == 0) & (offsets[None, :] == -1)
    keep_slot = keep_slot | (local_pos == TILES_DEV - 1) & (offsets[None, :] == 1)
    keep_slot = keep_slot & (candidates >= 0) & (candidates < TILES)
    marked = jnp.where(keep_slot, candidates, TILES + NB)
    ordered = jnp.sort(marked, axis=1)
    return jnp.where(ordered >= TILES, -1, ordered).astype(jnp.int32)


def raised(array, key, source, target, parts, factor):
    owner, partner = [(jnp.arange(array.shape[dim]) // (array.shape[dim] // parts)).reshape([-1 if axis == dim else 1 for axis in range(array.ndim)]) for dim in (source, target)]
    chosen = jax.random.permutation(key, parts)[partner]
    strong = (owner == chosen) | (owner == (partner + parts // 2) % parts)
    return jnp.where(strong, factor * array, array)


def levels(stream_key, extent, shards, least, largest):
    gain, own = 1.0, jax.random.fold_in(stream_key, 6)
    for axis_at, shards_of in shards:
        heights = jnp.exp(jax.random.uniform(jax.random.fold_in(own, axis_at), (shards_of,), jnp.float32, least / len(shards), largest / len(shards)))
        gain = gain * jnp.repeat(heights, extent[axis_at] // shards_of).reshape([-1 if axis == axis_at else 1 for axis in range(len(extent))])
    return gain


def noise(stream_key, extent, scale, most, shards=(), held_as=jnp.bfloat16):
    level = levels(stream_key, extent, shards, -0.22, 0.18) if shards else 1.0
    entries = jax.random.normal(stream_key, extent, jnp.float32) * scale * level
    return jnp.minimum(jnp.maximum(entries, -most), most).astype(held_as)


def gaussian_with(stream_key, dims, width, most, pieces, heavy, held_as=jnp.bfloat16):
    entries = width * jax.random.normal(stream_key, dims, jnp.float32)
    if pieces:
        entries = entries * levels(stream_key, dims, pieces, -0.22, 0.18)
    return jnp.clip(raised(entries, jax.random.fold_in(stream_key, 3), *heavy), -most, most).astype(held_as)


def setup_inputs(seed: int = 0) -> dict:
    key_list = jax.random.split(jax.random.key(seed), 7)
    return {
        "queries": draw_queries(jax.random.fold_in(key_list[6], 71), 0),
        "keys": draw_keys(jax.random.fold_in(key_list[6], 71), 0),
        "values": noise(key_list[2], (TOKENS, D), 1.0, 6.0, ((0, 32), (1, 8))),
        "w_out": noise(key_list[3], (D, D), D ** -0.5, 0.109375, ((0, 8), (1, 32))),
        "grad_out": gaussian_with(key_list[4], (TOKENS, D), 1.0, 6.0, ((0, 32), (1, 8)), (0, 1, 32, 2.75)),
        "neighbors": draw_neighbors(jax.random.fold_in(key_list[6], 71), 0),
    }


NEG_FILL = -1e+30

def reference(queries, keys, values, w_out, grad_out, neighbors):
    score_scale = 1.0 / math.sqrt(HD)
    tiled_q = queries.reshape(TILES, TILE, H, HD)
    tiled_k = keys.reshape(TILES, TILE, H, HD)
    tiled_v = values.reshape(TILES, TILE, H, HD)

    def gather_tiles(tile_table, tile_row):
        tile_slots = jnp.maximum(tile_row, 0).astype(jnp.int32)
        return tile_table[tile_slots].reshape(NB * TILE, H, HD)

    def tile_scores(tile_index):
        tile_row = neighbors[tile_index]
        allowed = jnp.repeat(tile_row >= 0, TILE)[None, None, :]
        key_rows = gather_tiles(tiled_k, tile_row)
        raw_scores = jnp.einsum('qhd,khd->hqk', tiled_q[tile_index].astype(jnp.float32), key_rows.astype(jnp.float32)) * score_scale
        return (jnp.where(allowed, raw_scores, NEG_FILL), tile_row)

    def forward_tile(tile_index):
        scores, tile_row = tile_scores(tile_index)
        row_top = lax.optimization_barrier(jnp.max(scores, axis=2, keepdims=True))
        log_total = row_top + jnp.log(lax.optimization_barrier(jnp.sum(jnp.exp(scores - row_top), axis=2, keepdims=True)))
        attn_probs = jnp.exp(scores - log_total).astype(jnp.bfloat16)
        value_rows = gather_tiles(tiled_v, tile_row)
        attended_tile = jnp.einsum('hqk,khd->qhd', attn_probs.astype(jnp.float32), value_rows.astype(jnp.float32)).astype(jnp.bfloat16)
        return (attended_tile, log_total[:, :, 0])
    attended_tiles, totals = lax.map(forward_tile, jnp.arange(TILES, dtype=jnp.int32))
    attended = attended_tiles.reshape(TOKENS, D)
    output = jnp.dot(attended, w_out, preferred_element_type=jnp.float32).astype(jnp.bfloat16)
    grad_attended = jnp.dot(grad_out, w_out.T, preferred_element_type=jnp.float32).astype(jnp.bfloat16)
    grad_weight = jnp.dot(attended.T, grad_out, preferred_element_type=jnp.float32)
    grad_tiles = grad_attended.reshape(TILES, TILE, H, HD)
    deltas = lax.optimization_barrier(jnp.sum(grad_tiles.astype(jnp.float32) * attended_tiles.astype(jnp.float32), axis=3))

    def backward_tile(carried, tile_index):
        key_acc, value_acc = carried
        scores, tile_row = tile_scores(tile_index)
        exact_probs = jnp.exp(scores - totals[tile_index][:, :, None])
        attn_probs = exact_probs.astype(jnp.bfloat16)
        key_rows = gather_tiles(tiled_k, tile_row)
        value_rows = gather_tiles(tiled_v, tile_row)
        grad_tile = grad_tiles[tile_index].astype(jnp.float32)
        inner_prod = jnp.einsum('qhd,khd->hqk', grad_tile, value_rows.astype(jnp.float32))
        grad_scores = (exact_probs * (inner_prod - deltas[tile_index].T[:, :, None]) * score_scale).astype(jnp.bfloat16)
        query_grad = jnp.einsum('hqk,khd->qhd', grad_scores.astype(jnp.float32), key_rows.astype(jnp.float32)).astype(jnp.bfloat16)
        key_part = jnp.einsum('hqk,qhd->khd', grad_scores.astype(jnp.float32), tiled_q[tile_index].astype(jnp.float32)).reshape(NB, TILE, H, HD)
        value_part = jnp.einsum('hqk,qhd->khd', attn_probs.astype(jnp.float32), grad_tile).reshape(NB, TILE, H, HD)
        tile_slots = jnp.maximum(tile_row, 0).astype(jnp.int32)
        key_acc = key_acc.at[tile_slots].add(key_part)
        value_acc = value_acc.at[tile_slots].add(value_part)
        return ((key_acc, value_acc), query_grad)
    zeros_acc = jnp.zeros((TILES, TILE, H, HD), jnp.float32)
    (key_acc, value_acc), query_grads = lax.scan(backward_tile, (zeros_acc, zeros_acc), jnp.arange(TILES, dtype=jnp.int32))
    grad_queries = query_grads.reshape(TOKENS, D)
    grad_keys = key_acc.reshape(TOKENS, D).astype(jnp.bfloat16)
    grad_values = value_acc.reshape(TOKENS, D).astype(jnp.bfloat16)
    return (output, grad_queries, grad_keys, grad_values, grad_weight)
```

```python
import math

import jax
import jax.numpy as jnp
from jax import lax
from jax.experimental import pallas as pl
from jax.experimental.pallas import tpu as pltpu
from jax.sharding import PartitionSpec as P

HD = 128
TILE = 384
HEADS = 3
TOK = 768
COLS = 384
WIN = 5 * TILE
WIDE = 6 * TILE
PIECE = 96
MESH = pl.DeviceIdType.MESH
SCALE = 1.0 / math.sqrt(HD)
LOG2E = 1.4426950408889634
NEG_FILL = -1e30
BF = jnp.bfloat16
F32 = jnp.float32


def dot_nn(a, b):
    return lax.dot_general(a, b, (((1,), (0,)), ((), ())), preferred_element_type=F32)


def dot_nt(a, b):
    return lax.dot_general(a, b, (((1,), (1,)), ((), ())), preferred_element_type=F32)


def dot_tn(a, b):
    return lax.dot_general(a, b, (((0,), (0,)), ((), ())), preferred_element_type=F32)


def aligned(start, size):
    return pl.ds(pl.multiple_of(start, size), size)


def kernel(
    nb_ref, q_ref, k_ref, v_ref, w_ref, go_ref,
    out_ref, gq_ref, gk_ref, gv_ref, gw_ref,
    kw, vw, gall, wt, att, scores, probs, inv_total,
    gsend, grecv, gown, gatt,
    osend, orecv, oown,
    gw, cs, cr, rs_s, rs_r, ls_s, ls_r, ys, yr,
    dka, dva, hs, hr,
    local_sem, wy_s, wy_r, wr_s, wr_r, wl_s, wl_r, wc_s, wc_r,
    kv_s, kv_r, ga_s, ga_r, at_s, at_r, gr_s, gr_r, or_s, or_r,
    gc_s, gc_r, gright_s, gright_r, gleft_s, gleft_r, gy_s, gy_r, hk_s, hk_r,
):
    f = lax.axis_index("fsdp")
    s = lax.axis_index("sp")
    ylo, x = f // 4, f % 4
    yhi, z, core = s // 16, (s // 2) % 8, s % 2

    def device(ylo_at, x_at, yhi_at, z_at, core_at):
        return (ylo_at * 4 + x_at, yhi_at * 16 + z_at * 2 + core_at)

    z_next = device(ylo, x, yhi, (z + 1) % 8, core)
    z_prev = device(ylo, x, yhi, (z + 7) % 8, core)
    partner = device(ylo, x, yhi, z, 1 - core)
    y_partner = device(1 - ylo, x, yhi, z, core)
    sp_next = (f, (s + 1) % 32)
    sp_prev = (f, (s + 31) % 32)

    def x_at(k):
        return device(ylo, (x + k) % 4, yhi, z, core)

    def remote(src, dst, send, recv, to):
        return pltpu.make_async_remote_copy(
            src_ref=src, dst_ref=dst, send_sem=send, recv_sem=recv, device_id=to, device_id_type=MESH
        )

    barrier = pltpu.get_barrier_semaphore()
    greeted = [
        z_next, z_prev, partner, sp_next, sp_prev, y_partner,
        device(ylo, x, 1 - yhi, z, core), device(1 - ylo, x, 1 - yhi, z, core),
        x_at(1), x_at(2), x_at(3),
    ]
    for other in greeted:
        pl.semaphore_signal(barrier, inc=1, device_id=other, device_id_type=MESH)
    pl.semaphore_wait(barrier, len(greeted))

    def slot(z_at, core_at):
        return pl.ds(pl.multiple_of((z_at * 2 + core_at) * PIECE, 32), PIECE)

    w_lanes = aligned(ylo * COLS, 128 * 3)

    def w_out_copy(k):
        return remote(
            w_ref, wt.at[slot(z, core), w_lanes], wy_s.at[k], wy_r.at[ylo], device(yhi, x, k, z, core)
        )

    def w_self_copy():
        return pltpu.make_async_copy(w_ref, wt.at[slot(z, core), w_lanes], local_sem.at[0])

    same = ylo == yhi
    for k in range(2):
        to_self = jnp.logical_and(same, yhi == k)

        @pl.when(jnp.logical_not(to_self))
        def _():
            w_out_copy(k).start()

    @pl.when(same)
    def _():
        w_self_copy().start()

    def lanes(h):
        return aligned(h * HD, HD)

    def kv_copies(h):
        made = []
        for i, (src, dst) in enumerate(((k_ref, kw), (v_ref, vw))):
            made.append(remote(
                src.at[:, lanes(h)], dst.at[pl.ds(0, TOK), lanes(h)],
                kv_s.at[h, 2 * i], kv_r.at[h, 2 * i], sp_next))
            made.append(remote(
                src.at[:, lanes(h)], dst.at[pl.ds(2 * TOK, TOK), lanes(h)],
                kv_s.at[h, 2 * i + 1], kv_r.at[h, 2 * i + 1], sp_prev))
        return made

    for copy in kv_copies(0):
        copy.start()

    def go_copy(t, k):
        return remote(
            go_ref.at[aligned(t * TILE, TILE), :], gall.at[aligned(t * TILE, TILE), aligned(x * COLS, COLS)],
            ga_s.at[t, k - 1], ga_r.at[t, k - 1], x_at(k))

    for t in range(2):
        for k in range(1, 4):
            go_copy(t, k).start()
    for h in range(1, HEADS):
        for copy in kv_copies(h):
            copy.start()

    own = pl.ds(TOK, TOK)
    locals_in = [
        pltpu.make_async_copy(k_ref, kw.at[own, :], local_sem.at[1]),
        pltpu.make_async_copy(v_ref, vw.at[own, :], local_sem.at[2]),
        pltpu.make_async_copy(go_ref, gall.at[:, aligned(x * COLS, COLS)], local_sem.at[3]),
    ]
    for copy in locals_in:
        copy.start()
    for copy in locals_in:
        copy.wait()

    def w_right(i):
        at = wt.at[slot((z + 8 - i) % 8, core), :]
        return remote(at, at, wr_s.at[i], wr_r.at[i], z_next)

    def w_left(i):
        at = wt.at[slot((z + i) % 8, core), :]
        return remote(at, at, wl_s.at[i], wl_r.at[i], z_prev)

    def w_core(i, z_at):
        at = wt.at[slot(z_at, core), :]
        return remote(at, at, wc_s.at[i], wc_r.at[i], partner)

    def w_ring_start():
        @pl.when(same)
        def _():
            w_self_copy().wait()

        for i in range(2):
            from_self = jnp.logical_and(same, ylo == i)

            @pl.when(jnp.logical_not(from_self))
            def _():
                remote(
                    w_ref, wt.at[slot(z, core), pl.ds(i * COLS, COLS)], wy_s.at[0], wy_r.at[i], partner
                ).wait_recv()

        w_right(0).start()
        w_left(0).start()
        w_core(0, z).start()

    def w_ring_step(i):
        w_right(i - 1).wait_recv()
        if i < 4:
            w_right(i).start()
        w_core(i, (z + 8 - i) % 8).start()
        if i < 4:
            w_left(i - 1).wait_recv()
            if i < 3:
                w_left(i).start()
            w_core(4 + i, (z + i) % 8).start()

    w_ring_start()

    first = s * 2 - 2

    def forward(h, t):
        rows = aligned(t * TILE, TILE)
        query = q_ref[rows, lanes(h)]
        top = jnp.full((1, TILE), -3e38, F32)
        for j in range(5):
            tile_id = first + t + j
            hit = nb_ref[t, 0] == tile_id
            for i in range(1, 5):
                hit = jnp.logical_or(hit, nb_ref[t, i] == tile_id)
            hit = jnp.logical_and(hit, tile_id >= 0)
            bias = jnp.where(hit, 0.0, NEG_FILL)
            key = kw[aligned((t + j) * TILE, TILE), lanes(h)]
            block = dot_nt(key, query) * (SCALE * LOG2E) + bias
            scores[pl.ds(j * TILE, TILE), :] = block
            top = jnp.maximum(top, jnp.max(block, axis=0, keepdims=True))
        total = jnp.zeros((1, TILE), F32)
        u = h * 2 + t
        for j in range(5):
            e = jnp.exp2(scores[pl.ds(j * TILE, TILE), :] - top)
            total = total + jnp.sum(e, axis=0, keepdims=True)
            probs[u, pl.ds(j * TILE, TILE), :] = e.astype(BF)
        turned = dot_tn(
            vw[pl.ds(pl.multiple_of(t * TILE, TILE), WIN), lanes(h)], probs[u]
        )
        inv = 1.0 / total
        inv_total[u] = inv
        att[rows, pl.ds(pl.multiple_of(ylo * COLS + h * HD, HD), HD)] = (turned * inv).T.astype(BF)

    def att_copy(h):
        at = att.at[:, pl.ds(pl.multiple_of(ylo * COLS + h * HD, HD), HD)]
        return remote(at, at, at_s.at[h], at_r.at[h], y_partner)

    def fwd_step(u, carry):
        h, t = u // 2, u % 2

        @pl.when(t == 0)
        def _():
            for copy in kv_copies(h):
                copy.wait_recv()

        for i in range(1, 3):
            @pl.when(u == 2 * i)
            def _():
                w_ring_step(i)

        forward(h, t)

        @pl.when(t == 1)
        def _():
            att_copy(h).start()

        return carry

    lax.fori_loop(0, 2 * HEADS, fwd_step, 0)
    w_ring_step(3)
    w_ring_step(4)
    for i in range(8):
        w_core(i, z).wait_recv()

    def gr_copy(t):
        rows = aligned(t * TILE, TILE)
        return remote(gsend.at[rows, :], grecv.at[rows, :], gr_s.at[t], gr_r.at[t], y_partner)

    def grad_step(t, carry):
        rows = aligned(t * TILE, TILE)
        for k in range(1, 4):
            go_copy(t, k).wait_recv()
        block = gall[rows, :]
        gsend[rows, :] = dot_nn(block, wt[:, aligned((1 - ylo) * COLS, COLS)]).astype(BF)
        gr_copy(t).start()
        gown[rows, :] = dot_nn(block, wt[:, aligned(ylo * COLS, COLS)])
        return carry

    lax.fori_loop(0, 2, grad_step, 0)

    def out_copy(t, k):
        rows = aligned(t * TILE, TILE)
        return remote(
            osend.at[k - 1, rows, :], orecv.at[k - 1, rows, :], or_s.at[t, k - 1], or_r.at[t, k - 1], x_at(k))

    for h in range(HEADS):
        att_copy(h).wait_recv()

    def out_step(t, carry):
        rows = aligned(t * TILE, TILE)
        block = att[rows, :]

        def out_part(k, inner):
            osend[k - 1, rows, :] = dot_nt(block, wt[aligned(((x + k) % 4) * COLS, COLS), :]).astype(BF)
            out_copy(t, k).start()
            return inner

        lax.fori_loop(1, 4, out_part, 0)
        oown[rows, :] = dot_nt(block, wt[aligned(x * COLS, COLS), :])
        return carry

    lax.fori_loop(0, 2, out_step, 0)

    def gw_step(i, carry):
        part = dot_tn(gall[:, aligned(i * COLS, COLS)], att[...])
        gw[pl.ds(i * 4, 4)] = part.reshape(4, PIECE, 2 * COLS)
        return carry

    lax.fori_loop(0, 4, gw_step, 0)

    def gw_cast(i, carry):
        cs[i] = gw[i * 2 + 1 - core].astype(BF)
        return carry

    lax.fori_loop(0, 8, gw_cast, 0)
    core_copy = remote(cs, cr, gc_s, gc_r, partner)
    core_copy.start()

    def g_right(i):
        return remote(rs_s.at[i], rs_r.at[i], gright_s.at[i], gright_r.at[i], z_next)

    def g_left(i):
        return remote(ls_s.at[i], ls_r.at[i], gleft_s.at[i], gleft_r.at[i], z_prev)

    def chip_sum(z_at):
        return gw[z_at * 2 + core] + cr[z_at].astype(F32)

    def g_ring_step(i):
        if i == 0:
            core_copy.wait_recv()
        if i > 0:
            g_right(i - 1).wait_recv()
        if i < 4:
            mine = chip_sum((z + 4 - i) % 8)
            if i > 0:
                mine = mine + rs_r[i - 1].astype(F32)
            rs_s[i] = mine.astype(BF)
            g_right(i).start()
        if 0 < i < 4:
            g_left(i - 1).wait_recv()
        if i < 3:
            mine = chip_sum((z + 5 + i) % 8)
            if i > 0:
                mine = mine + ls_r[i - 1].astype(F32)
            ls_s[i] = mine.astype(BF)
            g_left(i).start()

    def halo_copies(h):
        made = []
        for i in range(4):
            made.append(remote(
                hs.at[i, :, lanes(h)], hr.at[i, :, lanes(h)], hk_s.at[h, i], hk_r.at[h, i],
                sp_prev if i < 2 else sp_next))
        return made

    def backward(h, t):
        rows = pl.ds(t * TILE, TILE)
        u = h * 2 + t
        query = q_ref[rows, lanes(h)]
        grad = gatt[rows, lanes(h)]
        made = att[rows, pl.ds(pl.multiple_of(ylo * COLS + h * HD, HD), HD)]
        delta = jnp.sum((grad.astype(F32) * made.astype(F32)).T, axis=0, keepdims=True)
        inv = inv_total[u]
        factor = inv * SCALE
        shift = delta * factor
        inv_rows = jnp.broadcast_to(inv, (HD, TILE)).T
        grad_scaled = (grad.astype(F32) * inv_rows).astype(BF)
        turned = jnp.zeros((HD, TILE), F32)
        for j in range(5):
            at = pl.ds((t + j) * TILE, TILE)
            key = kw[at, lanes(h)]
            value = vw[at, lanes(h)]
            prob = probs[u, pl.ds(j * TILE, TILE), :]
            inner = dot_nt(value, grad)
            ds = (prob.astype(F32) * (inner * factor - shift)).astype(BF)
            dk = dot_nn(ds, query)
            dv = dot_nn(prob, grad_scaled)
            if t == 0 or j == 4:
                dka[at, lanes(h)] = dk
                dva[at, lanes(h)] = dv
            else:
                dka[at, lanes(h)] += dk
                dva[at, lanes(h)] += dv
            turned = turned + dot_tn(key, ds)
        gq_ref[rows, lanes(h)] = turned.T.astype(BF)

    for t in range(2):
        gr_copy(t).wait_recv()
        rows = pl.ds(t * TILE, TILE)
        gatt[rows, :] = (gown[rows, :] + grecv[rows, :].astype(F32)).astype(BF)

        def bwd_step(h, carry):
            if t == 0:
                for i in range(0, 3):
                    @pl.when(h == i)
                    def _():
                        g_ring_step(i)
            else:
                for i in range(3, 5):
                    @pl.when(h == i - 2)
                    def _():
                        g_ring_step(i)

            backward(h, t)
            if t == 1:
                hs[0, :, lanes(h)] = dka[pl.ds(0, TOK), lanes(h)].astype(BF)
                hs[1, :, lanes(h)] = dva[pl.ds(0, TOK), lanes(h)].astype(BF)
                hs[2, :, lanes(h)] = dka[pl.ds(2 * TOK, TOK), lanes(h)].astype(BF)
                hs[3, :, lanes(h)] = dva[pl.ds(2 * TOK, TOK), lanes(h)].astype(BF)
                for copy in halo_copies(h):
                    copy.start()
            return carry

        lax.fori_loop(0, HEADS, bwd_step, 0)

    z_sum = chip_sum(z) + rs_r[3].astype(F32) + ls_r[2].astype(F32)
    ys[0] = z_sum[:, :COLS]
    ys[1] = z_sum[:, COLS:]

    def gy_copy(i):
        return remote(ys.at[i], yr.at[yhi], gy_s.at[i], gy_r.at[yhi], device(i, x, ylo, z, core))

    def gy_self():
        return pltpu.make_async_copy(ys.at[ylo], yr.at[yhi], local_sem.at[4])

    for i in range(2):
        to_self = jnp.logical_and(same, ylo == i)

        @pl.when(jnp.logical_not(to_self))
        def _():
            gy_copy(i).start()

    @pl.when(same)
    def _():
        gy_self().start()

    for t in range(2):
        for k in range(1, 4):
            out_copy(t, k).wait_recv()
    out_ref[...] = (
        oown[...] + orecv[0].astype(F32) + orecv[1].astype(F32) + orecv[2].astype(F32)
    ).astype(BF)

    @pl.when(same)
    def _():
        gy_self().wait()

    for i in range(2):
        from_self = jnp.logical_and(same, yhi == i)

        @pl.when(jnp.logical_not(from_self))
        def _():
            remote(ys.at[i], yr.at[i], gy_s.at[i], gy_r.at[i], partner).wait_recv()

    gw_ref[...] = yr[0] + yr[1]

    for h in range(HEADS):
        for copy in halo_copies(h):
            copy.wait_recv()
        at = pl.ds(h * HD, HD)
        gk_ref[:, at] = (
            dka[own, at] + hr[0, :, at].astype(F32) + hr[2, :, at].astype(F32)
        ).astype(BF)
        gv_ref[:, at] = (
            dva[own, at] + hr[1, :, at].astype(F32) + hr[3, :, at].astype(F32)
        ).astype(BF)

    for k in range(2):
        to_self = jnp.logical_and(same, yhi == k)

        @pl.when(jnp.logical_not(to_self))
        def _():
            w_out_copy(k).wait_send()

    for i in range(2):
        to_self = jnp.logical_and(same, ylo == i)

        @pl.when(jnp.logical_not(to_self))
        def _():
            gy_copy(i).wait_send()

    for h in range(HEADS):
        for copy in kv_copies(h) + halo_copies(h) + [att_copy(h)]:
            copy.wait_send()
    for t in range(2):
        gr_copy(t).wait_send()
        for k in range(1, 4):
            go_copy(t, k).wait_send()
            out_copy(t, k).wait_send()
    for i in range(4):
        w_right(i).wait_send()
        g_right(i).wait_send()
    for i in range(3):
        w_left(i).wait_send()
        g_left(i).wait_send()
    for i in range(8):
        w_core(i, z).wait_send()
    core_copy.wait_send()


def local(queries, keys, values, w_out, grad_out, neighbors):
    vmem = lambda shape, dtype: pltpu.VMEM(shape, dtype)
    dma = lambda *shape: pltpu.SemaphoreType.DMA(shape)
    big = jax.ShapeDtypeStruct((TOK, COLS), BF)
    anywhere = pl.BlockSpec(memory_space=pl.ANY)
    whole = pl.BlockSpec(memory_space=pltpu.VMEM)
    out, gq, gk, gv, gwt = pl.pallas_call(
        kernel,
        out_shape=(big, big, big, big, jax.ShapeDtypeStruct((PIECE, COLS), F32)),
        in_specs=[pl.BlockSpec(memory_space=pltpu.SMEM), whole, anywhere, anywhere, anywhere, anywhere],
        out_specs=[whole] * 5,
        scratch_shapes=[
            vmem((WIDE, COLS), BF), vmem((WIDE, COLS), BF),
            vmem((TOK, 4 * COLS), BF), vmem((4 * COLS, 2 * COLS), BF), vmem((TOK, 2 * COLS), BF),
            vmem((WIN, TILE), F32), vmem((2 * HEADS, WIN, TILE), BF), vmem((2 * HEADS, 1, TILE), F32),
            vmem((TOK, COLS), BF), vmem((TOK, COLS), BF), vmem((TOK, COLS), F32), vmem((TOK, COLS), BF),
            vmem((3, TOK, COLS), BF), vmem((3, TOK, COLS), BF), vmem((TOK, COLS), F32),
            vmem((16, PIECE, 2 * COLS), F32),
            vmem((8, PIECE, 2 * COLS), BF), vmem((8, PIECE, 2 * COLS), BF),
            vmem((4, PIECE, 2 * COLS), BF), vmem((4, PIECE, 2 * COLS), BF),
            vmem((3, PIECE, 2 * COLS), BF), vmem((3, PIECE, 2 * COLS), BF),
            vmem((2, PIECE, COLS), F32), vmem((2, PIECE, COLS), F32),
            vmem((WIDE, COLS), F32), vmem((WIDE, COLS), F32),
            vmem((4, TOK, COLS), BF), vmem((4, TOK, COLS), BF),
            dma(5), dma(2), dma(2), dma(4), dma(4), dma(3), dma(3), dma(8), dma(8),
            dma(3, 4), dma(3, 4), dma(2, 3), dma(2, 3), dma(3), dma(3), dma(2), dma(2), dma(2, 3), dma(2, 3),
            pltpu.SemaphoreType.DMA, pltpu.SemaphoreType.DMA, dma(4), dma(4), dma(3), dma(3), dma(2), dma(2),
            dma(3, 4), dma(3, 4),
        ],
        compiler_params=pltpu.CompilerParams(
            collective_id=0, has_side_effects=True, vmem_limit_bytes=62 * 2**20
        ),
        name="block",
    )(neighbors, queries, keys, values, w_out.T, grad_out)
    return (out, gq, gk, gv, gwt.T)


def solution(mesh):
    placed = (
        P("sp", "fsdp"),
        P("sp", "fsdp"),
        P("sp", "fsdp"),
        P("fsdp", "sp"),
        P("sp", "fsdp"),
        P("sp", None),
    )
    return jax.shard_map(
        local,
        mesh=mesh,
        in_specs=placed,
        out_specs=(
            P("sp", "fsdp"),
            P("sp", "fsdp"),
            P("sp", "fsdp"),
            P("sp", "fsdp"),
            P("fsdp", "sp"),
        ),
        check_vma=False,
    )
```

```python
import math

import jax
import jax.numpy as jnp
from jax import lax
from jax.experimental import pallas as pl
from jax.experimental.pallas import tpu as pltpu
from jax.sharding import PartitionSpec as P

HD = 128
TILE = 384
HEADS = 3
TOK = 768
COLS = 384
WIN = 5 * TILE
WIDE = 6 * TILE
PIECE = 96
MESH = pl.DeviceIdType.MESH
SCALE = 1.0 / math.sqrt(HD)
LOG2E = 1.4426950408889634
NEG_FILL = -1e30
BF = jnp.bfloat16
F32 = jnp.float32


def dot_nn(a, b):
    return lax.dot_general(a, b, (((1,), (0,)), ((), ())), preferred_element_type=F32)


def dot_nt(a, b):
    return lax.dot_general(a, b, (((1,), (1,)), ((), ())), preferred_element_type=F32)


def dot_tn(a, b):
    return lax.dot_general(a, b, (((0,), (0,)), ((), ())), preferred_element_type=F32)


def aligned(start, size):
    return pl.ds(pl.multiple_of(start, size), size)


def kernel(
    nb_ref, q_ref, k_ref, v_ref, w_ref, go_ref,
    out_ref, gq_ref, gk_ref, gv_ref, gw_ref,
    kw, vw, gall, wt, att, scores, probs, inv_total,
    gsend, grecv, gown, gatt,
    osend, orecv, oown, held,
    gw, cs, cr, rs_s, rs_r, ls_s, ls_r, ys, yr,
    dka, dva, hs, hr,
    local_sem, wy_s, wy_r, wr_s, wr_r, wl_s, wl_r, wc_s, wc_r,
    kv_s, kv_r, ga_s, ga_r, gf_s, gf_r, at_s, at_r, gr_s, gr_r, or_s, or_r,
    gc_s, gc_r, gright_s, gright_r, gleft_s, gleft_r, gy_s, gy_r, hk_s, hk_r,
):
    f = lax.axis_index("fsdp")
    s = lax.axis_index("sp")
    ylo, x = f // 4, f % 4
    yhi, z, core = s // 16, (s // 2) % 8, s % 2

    def device(ylo_at, x_at, yhi_at, z_at, core_at):
        return (ylo_at * 4 + x_at, yhi_at * 16 + z_at * 2 + core_at)

    z_next = device(ylo, x, yhi, (z + 1) % 8, core)
    z_prev = device(ylo, x, yhi, (z + 7) % 8, core)
    partner = device(ylo, x, yhi, z, 1 - core)
    y_partner = device(1 - ylo, x, yhi, z, core)
    sp_next = (f, (s + 1) % 32)
    sp_prev = (f, (s + 31) % 32)

    def x_at(k):
        return device(ylo, (x + k) % 4, yhi, z, core)

    def remote(src, dst, send, recv, to):
        return pltpu.make_async_remote_copy(
            src_ref=src, dst_ref=dst, send_sem=send, recv_sem=recv, device_id=to, device_id_type=MESH
        )

    barrier = pltpu.get_barrier_semaphore()
    greeted = [
        z_next, z_prev, partner, sp_next, sp_prev, y_partner,
        device(ylo, x, 1 - yhi, z, core), device(1 - ylo, x, 1 - yhi, z, core),
        x_at(1), x_at(2), x_at(3),
    ]
    for other in greeted:
        pl.semaphore_signal(barrier, inc=1, device_id=other, device_id_type=MESH)
    pl.semaphore_wait(barrier, len(greeted))

    def slot(z_at, core_at):
        return pl.ds(pl.multiple_of((z_at * 2 + core_at) * PIECE, 32), PIECE)

    w_lanes = aligned(ylo * COLS, 128 * 3)

    def w_out_copy(k):
        return remote(
            w_ref, wt.at[slot(z, core), w_lanes], wy_s.at[k], wy_r.at[ylo], device(yhi, x, k, z, core)
        )

    def w_self_copy():
        return pltpu.make_async_copy(w_ref, wt.at[slot(z, core), w_lanes], local_sem.at[0])

    same = ylo == yhi
    for k in range(2):
        to_self = jnp.logical_and(same, yhi == k)

        @pl.when(jnp.logical_not(to_self))
        def _():
            w_out_copy(k).start()

    @pl.when(same)
    def _():
        w_self_copy().start()

    def lanes(h):
        return aligned(h * HD, HD)

    def kv_copies(h):
        made = []
        for i, (src, dst) in enumerate(((k_ref, kw), (v_ref, vw))):
            made.append(remote(
                src.at[:, lanes(h)], dst.at[pl.ds(0, TOK), lanes(h)],
                kv_s.at[h, 2 * i], kv_r.at[h, 2 * i], sp_next))
            made.append(remote(
                src.at[:, lanes(h)], dst.at[pl.ds(2 * TOK, TOK), lanes(h)],
                kv_s.at[h, 2 * i + 1], kv_r.at[h, 2 * i + 1], sp_prev))
        return made

    for copy in kv_copies(0):
        copy.start()

    def go_copy(t, left):
        rows = pl.ds(t * TILE, TILE)
        return remote(
            go_ref.at[rows, :], gall.at[rows, aligned(x * COLS, COLS)],
            ga_s.at[left, t], ga_r.at[left, t], x_at(3 if left else 1))

    def go_relay(left):
        at = gall.at[pl.ds(left * TILE, TILE), aligned((x + (1 if left else 3)) % 4 * COLS, COLS)]
        return remote(at, at, gf_s.at[left], gf_r.at[left], x_at(3 if left else 1))

    go_copy(0, 0).start()
    go_copy(1, 1).start()
    go_copy(1, 0).start()
    go_copy(0, 1).start()

    own = pl.ds(TOK, TOK)
    locals_in = [
        pltpu.make_async_copy(k_ref, kw.at[own, :], local_sem.at[1]),
        pltpu.make_async_copy(v_ref, vw.at[own, :], local_sem.at[2]),
        pltpu.make_async_copy(go_ref, gall.at[:, aligned(x * COLS, COLS)], local_sem.at[3]),
    ]
    for copy in locals_in:
        copy.start()
    for copy in locals_in:
        copy.wait()

    def w_right(i):
        at = wt.at[slot((z + 8 - i) % 8, core), :]
        return remote(at, at, wr_s.at[i], wr_r.at[i], z_next)

    def w_left(i):
        at = wt.at[slot((z + i) % 8, core), :]
        return remote(at, at, wl_s.at[i], wl_r.at[i], z_prev)

    def w_core(i, z_at):
        at = wt.at[slot(z_at, core), :]
        return remote(at, at, wc_s.at[i], wc_r.at[i], partner)

    def w_ring_start():
        @pl.when(same)
        def _():
            w_self_copy().wait()

        for i in range(2):
            from_self = jnp.logical_and(same, ylo == i)

            @pl.when(jnp.logical_not(from_self))
            def _():
                remote(
                    w_ref, wt.at[slot(z, core), pl.ds(i * COLS, COLS)], wy_s.at[0], wy_r.at[i], partner
                ).wait_recv()

        w_right(0).start()
        w_left(0).start()
        w_core(0, z).start()

    def w_ring_step(i):
        w_right(i - 1).wait_recv()
        if i < 4:
            w_right(i).start()
        w_core(i, (z + 8 - i) % 8).start()
        if i < 4:
            w_left(i - 1).wait_recv()
            if i < 3:
                w_left(i).start()
            w_core(4 + i, (z + i) % 8).start()

    w_ring_start()
    for copy in kv_copies(1):
        copy.start()

    first = s * 2 - 2

    def forward(h, t):
        rows = aligned(t * TILE, TILE)
        query = q_ref[rows, lanes(h)]
        top = jnp.full((1, TILE), -3e38, F32)
        for j in range(5):
            tile_id = first + t + j
            hit = nb_ref[t, 0] == tile_id
            for i in range(1, 5):
                hit = jnp.logical_or(hit, nb_ref[t, i] == tile_id)
            hit = jnp.logical_and(hit, tile_id >= 0)
            bias = jnp.where(hit, 0.0, NEG_FILL)
            key = kw[aligned((t + j) * TILE, TILE), lanes(h)]
            block = dot_nt(key, query) * (SCALE * LOG2E) + bias
            scores[pl.ds(j * TILE, TILE), :] = block
            top = jnp.maximum(top, jnp.max(block, axis=0, keepdims=True))
        total = jnp.zeros((1, TILE), F32)
        u = h * 2 + t
        for j in range(5):
            e = jnp.exp2(scores[pl.ds(j * TILE, TILE), :] - top)
            total = total + jnp.sum(e, axis=0, keepdims=True)
            probs[u, pl.ds(j * TILE, TILE), :] = e.astype(BF)
        turned = dot_tn(
            vw[pl.ds(pl.multiple_of(t * TILE, TILE), WIN), lanes(h)], probs[u]
        )
        inv = 1.0 / total
        inv_total[u] = inv
        att[rows, pl.ds(pl.multiple_of(ylo * COLS + h * HD, HD), HD)] = (turned * inv).T.astype(BF)

    def att_copy(h):
        at = att.at[:, pl.ds(pl.multiple_of(ylo * COLS + h * HD, HD), HD)]
        return remote(at, at, at_s.at[h], at_r.at[h], y_partner)

    def fwd_step(u, carry):
        h, t = u // 2, u % 2

        @pl.when(t == 0)
        def _():
            for copy in kv_copies(h):
                copy.wait_recv()

        @pl.when(u == 1)
        def _():
            w_ring_step(1)
            for copy in kv_copies(2):
                copy.start()

        @pl.when(u == 2)
        def _():
            go_copy(0, 0).wait_recv()
            go_relay(0).start()
            go_copy(1, 1).wait_recv()
            go_relay(1).start()

        for i in range(2, 4):
            @pl.when(u == 2 * i - 1)
            def _():
                w_ring_step(i)

        forward(h, t)

        @pl.when(t == 1)
        def _():
            att_copy(h).start()

        return carry

    lax.fori_loop(0, 2 * HEADS, fwd_step, 0)
    go_copy(1, 0).wait_recv()
    go_copy(0, 1).wait_recv()
    go_relay(0).wait_recv()
    go_relay(1).wait_recv()

    def gw_half(half):
        at = aligned(half * COLS, COLS)

        def gw_step(i, carry):
            part = dot_tn(gall[:, aligned(i * COLS, COLS)], att[:, at])
            gw[pl.ds(i * 4, 4), :, at] = part.reshape(4, PIECE, COLS)
            return carry

        lax.fori_loop(0, 4, gw_step, 0)

    gw_half(ylo)
    w_ring_step(4)
    for h in range(HEADS):
        att_copy(h).wait_recv()
    gw_half(1 - ylo)

    def gw_cast(i, carry):
        cs[i] = gw[i * 2 + 1 - core].astype(BF)
        return carry

    lax.fori_loop(0, 8, gw_cast, 0)
    core_copy = remote(cs, cr, gc_s, gc_r, partner)
    core_copy.start()
    for i in range(8):
        w_core(i, z).wait_recv()

    def g_right(i):
        return remote(rs_s.at[i], rs_r.at[i], gright_s.at[i], gright_r.at[i], z_next)

    def g_left(i):
        return remote(ls_s.at[i], ls_r.at[i], gleft_s.at[i], gleft_r.at[i], z_prev)

    def chip_sum(z_at):
        return gw[z_at * 2 + core] + cr[z_at].astype(F32)

    def g_ring_step(i):
        if i == 0:
            core_copy.wait_recv()
        if i > 0:
            g_right(i - 1).wait_recv()
        if i < 4:
            mine = chip_sum((z + 4 - i) % 8)
            if i > 0:
                mine = mine + rs_r[i - 1].astype(F32)
            rs_s[i] = mine.astype(BF)
            g_right(i).start()
        if 0 < i < 4:
            g_left(i - 1).wait_recv()
        if i < 3:
            mine = chip_sum((z + 5 + i) % 8)
            if i > 0:
                mine = mine + ls_r[i - 1].astype(F32)
            ls_s[i] = mine.astype(BF)
            g_left(i).start()

    def gr_copy(t):
        rows = aligned(t * TILE, TILE)
        return remote(gsend.at[rows, :], grecv.at[rows, :], gr_s.at[t], gr_r.at[t], y_partner)

    def grad_step(t, carry):
        rows = aligned(t * TILE, TILE)
        block = gall[rows, :]
        gsend[rows, :] = dot_nn(block, wt[:, aligned((1 - ylo) * COLS, COLS)]).astype(BF)
        gr_copy(t).start()
        gown[rows, :] = dot_nn(block, wt[:, aligned(ylo * COLS, COLS)])
        return carry

    lax.fori_loop(0, 2, grad_step, 0)
    g_ring_step(0)

    def out_copy(i):
        return remote(osend.at[i], orecv.at[i], or_s.at[i], or_r.at[i], x_at(1 if i < 3 else 3))

    def out_part(t, k):
        return dot_nt(att[pl.ds(t * TILE, TILE), :], wt[aligned((x + k) % 4 * COLS, COLS), :])

    def out_send(i, part):
        osend[i] = part.astype(BF)
        out_copy(i).start()

    out_send(0, out_part(0, 2))
    out_send(3, out_part(1, 2))
    out_send(5, out_part(0, 3))
    out_send(2, out_part(1, 1))
    held[0] = out_part(0, 1)
    held[1] = out_part(1, 3)

    def out_relay():
        for i in range(2):
            out_copy(3 * i).wait_recv()
            out_send(3 * i + 1, held[i] + orecv[3 * i].astype(F32))

    for t in range(2):
        oown[pl.ds(t * TILE, TILE), :] = out_part(t, 0)
    g_ring_step(1)

    def halo_copy(h, i):
        side, rows = ((0, pl.ds(0, TILE)), (0, pl.ds(TILE, TILE)), (1, pl.ds(0, TOK)))[i]
        return remote(
            hs.at[side, :, rows, lanes(h)], hr.at[side, :, rows, lanes(h)], hk_s.at[h, i], hk_r.at[h, i],
            sp_next if side else sp_prev)

    def halo_send(h, i):
        side, first_row, count = ((0, 0, TILE), (0, TILE, TILE), (1, 0, TOK))[i]
        to = pl.ds(first_row, count)
        at = pl.ds(side * 2 * TOK + first_row, count)
        hs[side, 0, to, lanes(h)] = dka[at, lanes(h)].astype(BF)
        hs[side, 1, to, lanes(h)] = dva[at, lanes(h)].astype(BF)
        halo_copy(h, i).start()

    def backward(h, t):
        rows = pl.ds(t * TILE, TILE)
        u = h * 2 + t
        query = q_ref[rows, lanes(h)]
        grad = gatt[rows, lanes(h)]
        made = att[rows, pl.ds(pl.multiple_of(ylo * COLS + h * HD, HD), HD)]
        delta = jnp.sum((grad.astype(F32) * made.astype(F32)).T, axis=0, keepdims=True)
        inv = inv_total[u]
        factor = inv * SCALE
        shift = delta * factor
        inv_rows = jnp.broadcast_to(inv, (HD, TILE)).T
        grad_scaled = (grad.astype(F32) * inv_rows).astype(BF)
        turned = jnp.zeros((HD, TILE), F32)
        for j in ((0, 1, 2, 3, 4), (0, 3, 4, 1, 2))[t]:
            at = pl.ds((t + j) * TILE, TILE)
            key = kw[at, lanes(h)]
            value = vw[at, lanes(h)]
            prob = probs[u, pl.ds(j * TILE, TILE), :]
            inner = dot_nt(value, grad)
            ds = (prob.astype(F32) * (inner * factor - shift)).astype(BF)
            dk = dot_nn(ds, query)
            dv = dot_nn(prob, grad_scaled)
            if t == 0 or j == 4:
                dka[at, lanes(h)] = dk
                dva[at, lanes(h)] = dv
            else:
                dka[at, lanes(h)] += dk
                dva[at, lanes(h)] += dv
            turned = turned + dot_tn(key, ds)
            if t == 0 and j == 0:
                halo_send(h, 0)
            if t == 1 and j == 4:
                halo_send(h, 1)
                halo_send(h, 2)
        gq_ref[rows, lanes(h)] = turned.T.astype(BF)

    def gy_copy(i):
        return remote(ys.at[i], yr.at[yhi], gy_s.at[i], gy_r.at[yhi], device(i, x, ylo, z, core))

    def gy_self():
        return pltpu.make_async_copy(ys.at[ylo], yr.at[yhi], local_sem.at[4])

    def gy_start():
        z_sum = chip_sum(z) + rs_r[3].astype(F32) + ls_r[2].astype(F32)
        ys[0] = z_sum[:, :COLS]
        ys[1] = z_sum[:, COLS:]
        for i in range(2):
            to_self = jnp.logical_and(same, ylo == i)

            @pl.when(jnp.logical_not(to_self))
            def _():
                gy_copy(i).start()

        @pl.when(same)
        def _():
            gy_self().start()

    for t in range(2):
        gr_copy(t).wait_recv()
        rows = pl.ds(t * TILE, TILE)
        gatt[rows, :] = (gown[rows, :] + grecv[rows, :].astype(F32)).astype(BF)

        def bwd_step(h, carry):
            if t == 0:
                @pl.when(h == 1)
                def _():
                    out_relay()

                @pl.when(h == 2)
                def _():
                    g_ring_step(2)
            else:
                @pl.when(h == 0)
                def _():
                    g_ring_step(3)

                @pl.when(h == 1)
                def _():
                    g_ring_step(4)
                    gy_start()

            backward(h, t)
            return carry

        lax.fori_loop(0, HEADS, bwd_step, 0)

    for i in (1, 2, 4, 5):
        out_copy(i).wait_recv()
    for t, i, j in ((0, 1, 5), (1, 4, 2)):
        rows = pl.ds(t * TILE, TILE)
        out_ref[rows, :] = (oown[rows, :] + orecv[i].astype(F32) + orecv[j].astype(F32)).astype(BF)

    @pl.when(same)
    def _():
        gy_self().wait()

    for i in range(2):
        from_self = jnp.logical_and(same, yhi == i)

        @pl.when(jnp.logical_not(from_self))
        def _():
            remote(ys.at[i], yr.at[i], gy_s.at[i], gy_r.at[i], partner).wait_recv()

    gw_ref[...] = yr[0] + yr[1]

    for h in range(HEADS):
        for i in range(3):
            halo_copy(h, i).wait_recv()
        at = pl.ds(h * HD, HD)
        gk_ref[:, at] = (
            dka[own, at] + hr[0, 0, :, at].astype(F32) + hr[1, 0, :, at].astype(F32)
        ).astype(BF)
        gv_ref[:, at] = (
            dva[own, at] + hr[0, 1, :, at].astype(F32) + hr[1, 1, :, at].astype(F32)
        ).astype(BF)

    for k in range(2):
        to_self = jnp.logical_and(same, yhi == k)

        @pl.when(jnp.logical_not(to_self))
        def _():
            w_out_copy(k).wait_send()

    for i in range(2):
        to_self = jnp.logical_and(same, ylo == i)

        @pl.when(jnp.logical_not(to_self))
        def _():
            gy_copy(i).wait_send()

    for h in range(HEADS):
        for copy in kv_copies(h) + [halo_copy(h, i) for i in range(3)] + [att_copy(h)]:
            copy.wait_send()
    for t in range(2):
        gr_copy(t).wait_send()
        go_copy(t, 0).wait_send()
        go_copy(t, 1).wait_send()
        go_relay(t).wait_send()
    for i in range(6):
        out_copy(i).wait_send()
    for i in range(4):
        w_right(i).wait_send()
        g_right(i).wait_send()
    for i in range(3):
        w_left(i).wait_send()
        g_left(i).wait_send()
    for i in range(8):
        w_core(i, z).wait_send()
    core_copy.wait_send()


def local(queries, keys, values, w_out, grad_out, neighbors):
    vmem = lambda shape, dtype: pltpu.VMEM(shape, dtype)
    dma = lambda *shape: pltpu.SemaphoreType.DMA(shape)
    big = jax.ShapeDtypeStruct((TOK, COLS), BF)
    anywhere = pl.BlockSpec(memory_space=pl.ANY)
    whole = pl.BlockSpec(memory_space=pltpu.VMEM)
    out, gq, gk, gv, gwt = pl.pallas_call(
        kernel,
        out_shape=(big, big, big, big, jax.ShapeDtypeStruct((PIECE, COLS), F32)),
        in_specs=[pl.BlockSpec(memory_space=pltpu.SMEM), whole, anywhere, anywhere, anywhere, anywhere],
        out_specs=[whole] * 5,
        scratch_shapes=[
            vmem((WIDE, COLS), BF), vmem((WIDE, COLS), BF),
            vmem((TOK, 4 * COLS), BF), vmem((4 * COLS, 2 * COLS), BF), vmem((TOK, 2 * COLS), BF),
            vmem((WIN, TILE), F32), vmem((2 * HEADS, WIN, TILE), BF), vmem((2 * HEADS, 1, TILE), F32),
            vmem((TOK, COLS), BF), vmem((TOK, COLS), BF), vmem((TOK, COLS), F32), vmem((TOK, COLS), BF),
            vmem((6, TILE, COLS), BF), vmem((6, TILE, COLS), BF), vmem((TOK, COLS), F32), vmem((2, TILE, COLS), F32),
            vmem((16, PIECE, 2 * COLS), F32),
            vmem((8, PIECE, 2 * COLS), BF), vmem((8, PIECE, 2 * COLS), BF),
            vmem((4, PIECE, 2 * COLS), BF), vmem((4, PIECE, 2 * COLS), BF),
            vmem((3, PIECE, 2 * COLS), BF), vmem((3, PIECE, 2 * COLS), BF),
            vmem((2, PIECE, COLS), F32), vmem((2, PIECE, COLS), F32),
            vmem((WIDE, COLS), F32), vmem((WIDE, COLS), F32),
            vmem((2, 2, TOK, COLS), BF), vmem((2, 2, TOK, COLS), BF),
            dma(5), dma(2), dma(2), dma(4), dma(4), dma(3), dma(3), dma(8), dma(8),
            dma(3, 4), dma(3, 4), dma(2, 2), dma(2, 2), dma(2), dma(2), dma(3), dma(3), dma(2), dma(2), dma(6), dma(6),
            pltpu.SemaphoreType.DMA, pltpu.SemaphoreType.DMA, dma(4), dma(4), dma(3), dma(3), dma(2), dma(2),
            dma(3, 3), dma(3, 3),
        ],
        compiler_params=pltpu.CompilerParams(
            collective_id=0, has_side_effects=True, vmem_limit_bytes=62 * 2**20
        ),
        name="block",
    )(neighbors, queries, keys, values, w_out.T, grad_out)
    return (out, gq, gk, gv, gwt.T)


def solution(mesh):
    placed = (
        P("sp", "fsdp"),
        P("sp", "fsdp"),
        P("sp", "fsdp"),
        P("fsdp", "sp"),
        P("sp", "fsdp"),
        P("sp", None),
    )
    return jax.shard_map(
        local,
        mesh=mesh,
        in_specs=placed,
        out_specs=(
            P("sp", "fsdp"),
            P("sp", "fsdp"),
            P("sp", "fsdp"),
            P("sp", "fsdp"),
            P("fsdp", "sp"),
        ),
        check_vma=False,
    )
```

```python
import math

import jax
import jax.numpy as jnp
from jax import lax
from jax.experimental import pallas as pl
from jax.experimental.pallas import tpu as pltpu
from jax.sharding import PartitionSpec as P

HD = 128
TILE = 384
HEADS = 3
TOK = 768
COLS = 384
WIN = 5 * TILE
WIDE = 6 * TILE
PIECE = 96
MESH = pl.DeviceIdType.MESH
SCALE = 1.0 / math.sqrt(HD)
LOG2E = 1.4426950408889634
NEG_FILL = -1e30
BF = jnp.bfloat16
F32 = jnp.float32


def dot_nn(a, b):
    return lax.dot_general(a, b, (((1,), (0,)), ((), ())), preferred_element_type=F32)


def dot_nt(a, b):
    return lax.dot_general(a, b, (((1,), (1,)), ((), ())), preferred_element_type=F32)


def dot_tn(a, b):
    return lax.dot_general(a, b, (((0,), (0,)), ((), ())), preferred_element_type=F32)


def aligned(start, size):
    return pl.ds(pl.multiple_of(start, size), size)


def kernel(
    nb_ref, q_ref, k_ref, v_ref, w_ref, go_ref,
    out_ref, gq_ref, gk_ref, gv_ref, gw_ref,
    kw, vw, gall, wt, att, scores, probs, inv_total,
    gsend, grecv, gown, gatt,
    osend, orecv, oown, held,
    gw, cs, cr, rs_s, rs_r, ls_s, ls_r, ys, yr,
    dka, dva, hs, hr,
    local_sem, wy_s, wy_r, wr_s, wr_r, wl_s, wl_r, wc_s, wc_r,
    kv_s, kv_r, ga_s, ga_r, gf_s, gf_r, at_s, at_r, gr_s, gr_r, or_s, or_r,
    gc_s, gc_r, gright_s, gright_r, gleft_s, gleft_r, gy_s, gy_r, hk_s, hk_r,
):
    f = lax.axis_index("fsdp")
    s = lax.axis_index("sp")
    ylo, x = f // 4, f % 4
    yhi, z, core = s // 16, (s // 2) % 8, s % 2

    def device(ylo_at, x_at, yhi_at, z_at, core_at):
        return (ylo_at * 4 + x_at, yhi_at * 16 + z_at * 2 + core_at)

    z_next = device(ylo, x, yhi, (z + 1) % 8, core)
    z_prev = device(ylo, x, yhi, (z + 7) % 8, core)
    partner = device(ylo, x, yhi, z, 1 - core)
    y_partner = device(1 - ylo, x, yhi, z, core)
    sp_next = (f, (s + 1) % 32)
    sp_prev = (f, (s + 31) % 32)

    def x_at(k):
        return device(ylo, (x + k) % 4, yhi, z, core)

    def remote(src, dst, send, recv, to):
        return pltpu.make_async_remote_copy(
            src_ref=src, dst_ref=dst, send_sem=send, recv_sem=recv, device_id=to, device_id_type=MESH
        )

    barrier = pltpu.get_barrier_semaphore()
    greeted = [
        z_next, z_prev, partner, sp_next, sp_prev, y_partner,
        device(ylo, x, 1 - yhi, z, core), device(1 - ylo, x, 1 - yhi, z, core),
        x_at(1), x_at(2), x_at(3),
    ]
    for other in greeted:
        pl.semaphore_signal(barrier, inc=1, device_id=other, device_id_type=MESH)
    pl.semaphore_wait(barrier, len(greeted))

    def slot(z_at, core_at):
        return pl.ds(pl.multiple_of((z_at * 2 + core_at) * PIECE, 32), PIECE)

    w_lanes = aligned(ylo * COLS, 128 * 3)

    def w_out_copy(k):
        return remote(
            w_ref, wt.at[slot(z, core), w_lanes], wy_s.at[k], wy_r.at[ylo], device(yhi, x, k, z, core)
        )

    def w_self_copy():
        return pltpu.make_async_copy(w_ref, wt.at[slot(z, core), w_lanes], local_sem.at[0])

    same = ylo == yhi
    for k in range(2):
        to_self = jnp.logical_and(same, yhi == k)

        @pl.when(jnp.logical_not(to_self))
        def _():
            w_out_copy(k).start()

    @pl.when(same)
    def _():
        w_self_copy().start()

    def lanes(h):
        return aligned(h * HD, HD)

    def kv_copies(h):
        made = []
        for i, (src, dst) in enumerate(((k_ref, kw), (v_ref, vw))):
            made.append(remote(
                src.at[:, lanes(h)], dst.at[pl.ds(0, TOK), lanes(h)],
                kv_s.at[h, 2 * i], kv_r.at[h, 2 * i], sp_next))
            made.append(remote(
                src.at[:, lanes(h)], dst.at[pl.ds(2 * TOK, TOK), lanes(h)],
                kv_s.at[h, 2 * i + 1], kv_r.at[h, 2 * i + 1], sp_prev))
        return made

    has_prev, has_next = s > 0, s < 31

    def kv_start(h):
        copies = kv_copies(h)

        @pl.when(has_next)
        def _():
            copies[0].start()
            copies[2].start()

        @pl.when(has_prev)
        def _():
            copies[1].start()
            copies[3].start()

    def kv_wait(h):
        copies = kv_copies(h)

        @pl.when(has_prev)
        def _():
            copies[0].wait_recv()
            copies[2].wait_recv()

        @pl.when(has_next)
        def _():
            copies[1].wait_recv()
            copies[3].wait_recv()

    kv_start(0)

    def go_copy(t, left):
        rows = pl.ds(t * TILE, TILE)
        return remote(
            go_ref.at[rows, :], gall.at[rows, aligned(x * COLS, COLS)],
            ga_s.at[left, t], ga_r.at[left, t], x_at(3 if left else 1))

    def go_relay(left):
        at = gall.at[pl.ds(left * TILE, TILE), aligned((x + (1 if left else 3)) % 4 * COLS, COLS)]
        return remote(at, at, gf_s.at[left], gf_r.at[left], x_at(3 if left else 1))

    go_copy(0, 0).start()
    go_copy(1, 1).start()
    go_copy(1, 0).start()
    go_copy(0, 1).start()

    own = pl.ds(TOK, TOK)
    for side, missing in ((0, s == 0), (1, s == 31)):
        @pl.when(missing)
        def _():
            outside = pl.ds(side * 2 * TOK, TOK)
            kw[outside, :] = jnp.zeros((TOK, COLS), BF)
            vw[outside, :] = jnp.zeros((TOK, COLS), BF)
            hr[1 - side] = jnp.zeros((2, TOK, COLS), BF)

    locals_in = [
        pltpu.make_async_copy(k_ref, kw.at[own, :], local_sem.at[1]),
        pltpu.make_async_copy(v_ref, vw.at[own, :], local_sem.at[2]),
        pltpu.make_async_copy(go_ref, gall.at[:, aligned(x * COLS, COLS)], local_sem.at[3]),
    ]
    for copy in locals_in:
        copy.start()
    for copy in locals_in:
        copy.wait()

    def w_right(i):
        at = wt.at[slot((z + 8 - i) % 8, core), :]
        return remote(at, at, wr_s.at[i], wr_r.at[i], z_next)

    def w_left(i):
        at = wt.at[slot((z + i) % 8, core), :]
        return remote(at, at, wl_s.at[i], wl_r.at[i], z_prev)

    def w_core(i, z_at):
        at = wt.at[slot(z_at, core), :]
        return remote(at, at, wc_s.at[i], wc_r.at[i], partner)

    def w_ring_start():
        @pl.when(same)
        def _():
            w_self_copy().wait()

        for i in range(2):
            from_self = jnp.logical_and(same, ylo == i)

            @pl.when(jnp.logical_not(from_self))
            def _():
                remote(
                    w_ref, wt.at[slot(z, core), pl.ds(i * COLS, COLS)], wy_s.at[0], wy_r.at[i], partner
                ).wait_recv()

        w_right(0).start()
        w_left(0).start()
        w_core(0, z).start()

    def w_ring_step(i):
        w_right(i - 1).wait_recv()
        if i < 4:
            w_right(i).start()
        w_core(i, (z + 8 - i) % 8).start()
        if i < 4:
            w_left(i - 1).wait_recv()
            if i < 3:
                w_left(i).start()
            w_core(4 + i, (z + i) % 8).start()

    w_ring_start()
    kv_start(1)

    first = s * 2 - 2

    def forward(h, t):
        rows = aligned(t * TILE, TILE)
        query = q_ref[rows, lanes(h)]
        top = jnp.full((1, TILE), -3e38, F32)
        for j in range(5):
            tile_id = first + t + j
            hit = nb_ref[t, 0] == tile_id
            for i in range(1, 5):
                hit = jnp.logical_or(hit, nb_ref[t, i] == tile_id)
            hit = jnp.logical_and(hit, tile_id >= 0)
            bias = jnp.where(hit, 0.0, NEG_FILL)
            key = kw[aligned((t + j) * TILE, TILE), lanes(h)]
            block = dot_nt(key, query) * (SCALE * LOG2E) + bias
            scores[pl.ds(j * TILE, TILE), :] = block
            top = jnp.maximum(top, jnp.max(block, axis=0, keepdims=True))
        total = jnp.zeros((1, TILE), F32)
        u = h * 2 + t
        for j in range(5):
            e = jnp.exp2(scores[pl.ds(j * TILE, TILE), :] - top)
            total = total + jnp.sum(e, axis=0, keepdims=True)
            probs[u, pl.ds(j * TILE, TILE), :] = e.astype(BF)
        turned = dot_tn(
            vw[pl.ds(pl.multiple_of(t * TILE, TILE), WIN), lanes(h)], probs[u]
        )
        inv = 1.0 / total
        inv_total[u] = inv
        att[rows, pl.ds(pl.multiple_of(ylo * COLS + h * HD, HD), HD)] = (turned * inv).T.astype(BF)

    def att_copy(h):
        at = att.at[:, pl.ds(pl.multiple_of(ylo * COLS + h * HD, HD), HD)]
        return remote(at, at, at_s.at[h], at_r.at[h], y_partner)

    def fwd_step(u, carry):
        h, t = u // 2, u % 2

        @pl.when(t == 0)
        def _():
            kv_wait(h)

        @pl.when(u == 1)
        def _():
            w_ring_step(1)
            kv_start(2)

        @pl.when(u == 2)
        def _():
            go_copy(0, 0).wait_recv()
            go_relay(0).start()
            go_copy(1, 1).wait_recv()
            go_relay(1).start()

        for i in range(2, 4):
            @pl.when(u == 2 * i - 1)
            def _():
                w_ring_step(i)

        forward(h, t)

        @pl.when(t == 1)
        def _():
            att_copy(h).start()

        return carry

    lax.fori_loop(0, 2 * HEADS, fwd_step, 0)
    go_copy(1, 0).wait_recv()
    go_copy(0, 1).wait_recv()
    go_relay(0).wait_recv()
    go_relay(1).wait_recv()

    def gw_half(half):
        at = aligned(half * COLS, COLS)

        def gw_step(i, carry):
            part = dot_tn(gall[:, aligned(i * COLS, COLS)], att[:, at])
            gw[pl.ds(i * 4, 4), :, at] = part.reshape(4, PIECE, COLS)
            return carry

        lax.fori_loop(0, 4, gw_step, 0)

    gw_half(ylo)
    w_ring_step(4)
    for i in range(8):
        w_core(i, z).wait_recv()

    def gr_copy(t):
        rows = aligned(t * TILE, TILE)
        return remote(gsend.at[rows, :], grecv.at[rows, :], gr_s.at[t], gr_r.at[t], y_partner)

    def grad_step(t, carry):
        rows = aligned(t * TILE, TILE)
        block = gall[rows, :]
        gsend[rows, :] = dot_nn(block, wt[:, aligned((1 - ylo) * COLS, COLS)]).astype(BF)
        gr_copy(t).start()
        gown[rows, :] = dot_nn(block, wt[:, aligned(ylo * COLS, COLS)])
        return carry

    lax.fori_loop(0, 2, grad_step, 0)
    for h in range(HEADS):
        att_copy(h).wait_recv()
    gw_half(1 - ylo)

    def gw_cast(i, carry):
        cs[i] = gw[i * 2 + 1 - core].astype(BF)
        return carry

    lax.fori_loop(0, 8, gw_cast, 0)
    core_copy = remote(cs, cr, gc_s, gc_r, partner)
    core_copy.start()
    def g_right(i):
        return remote(rs_s.at[i], rs_r.at[i], gright_s.at[i], gright_r.at[i], z_next)

    def g_left(i):
        return remote(ls_s.at[i], ls_r.at[i], gleft_s.at[i], gleft_r.at[i], z_prev)

    def chip_sum(z_at):
        return gw[z_at * 2 + core] + cr[z_at].astype(F32)

    def g_ring_step(i):
        if i == 0:
            core_copy.wait_recv()
        if i > 0:
            g_right(i - 1).wait_recv()
        if i < 4:
            mine = chip_sum((z + 4 - i) % 8)
            if i > 0:
                mine = mine + rs_r[i - 1].astype(F32)
            rs_s[i] = mine.astype(BF)
            g_right(i).start()
        if 0 < i < 4:
            g_left(i - 1).wait_recv()
        if i < 3:
            mine = chip_sum((z + 5 + i) % 8)
            if i > 0:
                mine = mine + ls_r[i - 1].astype(F32)
            ls_s[i] = mine.astype(BF)
            g_left(i).start()


    def out_copy(i):
        return remote(osend.at[i], orecv.at[i], or_s.at[i], or_r.at[i], x_at(1 if i < 3 else 3))

    def out_part(k):
        return dot_nt(att[...], wt[aligned((x + k) % 4 * COLS, COLS), :])

    def out_send(i, part):
        osend[i] = part.astype(BF)
        out_copy(i).start()

    part = out_part(2)
    out_send(0, part[:TILE])
    out_send(3, part[TILE:])
    part = out_part(3)
    out_send(5, part[:TILE])
    held[1] = part[TILE:]
    g_ring_step(0)
    part = out_part(1)
    out_send(2, part[TILE:])
    held[0] = part[:TILE]
    oown[...] = out_part(0)

    def out_relay():
        for i in range(2):
            out_copy(3 * i).wait_recv()
            out_send(3 * i + 1, held[i] + orecv[3 * i].astype(F32))


    def halo_copy(h, i):
        side, rows = ((0, pl.ds(0, TILE)), (0, pl.ds(TILE, TILE)), (1, pl.ds(0, TOK)))[i]
        return remote(
            hs.at[side, :, rows, lanes(h)], hr.at[side, :, rows, lanes(h)], hk_s.at[h, i], hk_r.at[h, i],
            sp_next if side else sp_prev)

    def halo_send(h, i):
        side, first_row, count = ((0, 0, TILE), (0, TILE, TILE), (1, 0, TOK))[i]
        to = pl.ds(first_row, count)
        at = pl.ds(side * 2 * TOK + first_row, count)

        @pl.when(has_next if side else has_prev)
        def _():
            hs[side, 0, to, lanes(h)] = dka[at, lanes(h)].astype(BF)
            hs[side, 1, to, lanes(h)] = dva[at, lanes(h)].astype(BF)
            halo_copy(h, i).start()

    def backward(h, t):
        rows = pl.ds(t * TILE, TILE)
        u = h * 2 + t
        query = q_ref[rows, lanes(h)]
        grad = gatt[rows, lanes(h)]
        made = att[rows, pl.ds(pl.multiple_of(ylo * COLS + h * HD, HD), HD)]
        delta = jnp.sum((grad.astype(F32) * made.astype(F32)).T, axis=0, keepdims=True)
        inv = inv_total[u]
        factor = inv * SCALE
        shift = delta * factor
        inv_rows = jnp.broadcast_to(inv, (HD, TILE)).T
        grad_scaled = (grad.astype(F32) * inv_rows).astype(BF)
        turned = jnp.zeros((HD, TILE), F32)
        for j in ((0, 1, 2, 3, 4), (0, 3, 4, 1, 2))[t]:
            at = pl.ds((t + j) * TILE, TILE)
            key = kw[at, lanes(h)]
            value = vw[at, lanes(h)]
            prob = probs[u, pl.ds(j * TILE, TILE), :]
            inner = dot_nt(value, grad)
            ds = (prob.astype(F32) * (inner * factor - shift)).astype(BF)
            dk = dot_nn(ds, query)
            dv = dot_nn(prob, grad_scaled)
            if t == 0 or j == 4:
                dka[at, lanes(h)] = dk
                dva[at, lanes(h)] = dv
            else:
                dka[at, lanes(h)] += dk
                dva[at, lanes(h)] += dv
            turned = turned + dot_tn(key, ds)
            if t == 0 and j == 0:
                halo_send(h, 0)
            if t == 1 and j == 4:
                halo_send(h, 1)
                halo_send(h, 2)
        gq_ref[rows, lanes(h)] = turned.T.astype(BF)

    def gy_copy(i):
        return remote(ys.at[i], yr.at[yhi], gy_s.at[i], gy_r.at[yhi], device(i, x, ylo, z, core))

    def gy_self():
        return pltpu.make_async_copy(ys.at[ylo], yr.at[yhi], local_sem.at[4])

    def gy_start():
        z_sum = chip_sum(z) + rs_r[3].astype(F32) + ls_r[2].astype(F32)
        ys[0] = z_sum[:, :COLS]
        ys[1] = z_sum[:, COLS:]
        for i in range(2):
            to_self = jnp.logical_and(same, ylo == i)

            @pl.when(jnp.logical_not(to_self))
            def _():
                gy_copy(i).start()

        @pl.when(same)
        def _():
            gy_self().start()

    for t in range(2):
        gr_copy(t).wait_recv()
        rows = pl.ds(t * TILE, TILE)
        gatt[rows, :] = (gown[rows, :] + grecv[rows, :].astype(F32)).astype(BF)

        def bwd_step(h, carry):
            if t == 0:
                @pl.when(h == 1)
                def _():
                    g_ring_step(1)

                @pl.when(h == 2)
                def _():
                    out_relay()
            else:
                @pl.when(h == 0)
                def _():
                    g_ring_step(2)

                @pl.when(h == 2)
                def _():
                    g_ring_step(3)

            backward(h, t)
            return carry

        lax.fori_loop(0, HEADS, bwd_step, 0)

    g_ring_step(4)
    gy_start()

    for i in (1, 2, 4, 5):
        out_copy(i).wait_recv()
    for t, i, j in ((0, 1, 5), (1, 4, 2)):
        rows = pl.ds(t * TILE, TILE)
        out_ref[rows, :] = (oown[rows, :] + orecv[i].astype(F32) + orecv[j].astype(F32)).astype(BF)

    for h in range(HEADS):
        @pl.when(has_next)
        def _():
            halo_copy(h, 0).wait_recv()
            halo_copy(h, 1).wait_recv()

        @pl.when(has_prev)
        def _():
            halo_copy(h, 2).wait_recv()

        at = pl.ds(h * HD, HD)
        gk_ref[:, at] = (
            dka[own, at] + hr[0, 0, :, at].astype(F32) + hr[1, 0, :, at].astype(F32)
        ).astype(BF)
        gv_ref[:, at] = (
            dva[own, at] + hr[0, 1, :, at].astype(F32) + hr[1, 1, :, at].astype(F32)
        ).astype(BF)

    @pl.when(same)
    def _():
        gy_self().wait()

    for i in range(2):
        from_self = jnp.logical_and(same, yhi == i)

        @pl.when(jnp.logical_not(from_self))
        def _():
            remote(ys.at[i], yr.at[i], gy_s.at[i], gy_r.at[i], partner).wait_recv()

    gw_ref[...] = yr[0] + yr[1]

    for k in range(2):
        to_self = jnp.logical_and(same, yhi == k)

        @pl.when(jnp.logical_not(to_self))
        def _():
            w_out_copy(k).wait_send()

    for i in range(2):
        to_self = jnp.logical_and(same, ylo == i)

        @pl.when(jnp.logical_not(to_self))
        def _():
            gy_copy(i).wait_send()

    for h in range(HEADS):
        copies = kv_copies(h)

        @pl.when(has_next)
        def _():
            for copy in (copies[0], copies[2], halo_copy(h, 2)):
                copy.wait_send()

        @pl.when(has_prev)
        def _():
            for copy in (copies[1], copies[3], halo_copy(h, 0), halo_copy(h, 1)):
                copy.wait_send()

        att_copy(h).wait_send()
    for t in range(2):
        gr_copy(t).wait_send()
        go_copy(t, 0).wait_send()
        go_copy(t, 1).wait_send()
        go_relay(t).wait_send()
    for i in range(6):
        out_copy(i).wait_send()
    for i in range(4):
        w_right(i).wait_send()
        g_right(i).wait_send()
    for i in range(3):
        w_left(i).wait_send()
        g_left(i).wait_send()
    for i in range(8):
        w_core(i, z).wait_send()
    core_copy.wait_send()


def deliver(*refs):
    for source, target in zip(refs[:5], refs[5:]):
        target[...] = source[...]


def local(queries, keys, values, w_out, grad_out, neighbors):
    vmem = lambda shape, dtype: pltpu.VMEM(shape, dtype)
    dma = lambda *shape: pltpu.SemaphoreType.DMA(shape)
    big = jax.ShapeDtypeStruct((TOK, COLS), BF)
    anywhere = pl.BlockSpec(memory_space=pl.ANY)
    whole = pl.BlockSpec(memory_space=pltpu.VMEM)
    out, gq, gk, gv, gwt = pl.pallas_call(
        kernel,
        out_shape=(big, big, big, big, jax.ShapeDtypeStruct((PIECE, COLS), F32)),
        in_specs=[pl.BlockSpec(memory_space=pltpu.SMEM), whole, anywhere, anywhere, anywhere, anywhere],
        out_specs=[whole] * 5,
        scratch_shapes=[
            vmem((WIDE, COLS), BF), vmem((WIDE, COLS), BF),
            vmem((TOK, 4 * COLS), BF), vmem((4 * COLS, 2 * COLS), BF), vmem((TOK, 2 * COLS), BF),
            vmem((WIN, TILE), F32), vmem((2 * HEADS, WIN, TILE), BF), vmem((2 * HEADS, 1, TILE), F32),
            vmem((TOK, COLS), BF), vmem((TOK, COLS), BF), vmem((TOK, COLS), F32), vmem((TOK, COLS), BF),
            vmem((6, TILE, COLS), BF), vmem((6, TILE, COLS), BF), vmem((TOK, COLS), F32), vmem((2, TILE, COLS), F32),
            vmem((16, PIECE, 2 * COLS), F32),
            vmem((8, PIECE, 2 * COLS), BF), vmem((8, PIECE, 2 * COLS), BF),
            vmem((4, PIECE, 2 * COLS), BF), vmem((4, PIECE, 2 * COLS), BF),
            vmem((3, PIECE, 2 * COLS), BF), vmem((3, PIECE, 2 * COLS), BF),
            vmem((2, PIECE, COLS), F32), vmem((2, PIECE, COLS), F32),
            vmem((WIDE, COLS), F32), vmem((WIDE, COLS), F32),
            vmem((2, 2, TOK, COLS), BF), vmem((2, 2, TOK, COLS), BF),
            dma(5), dma(2), dma(2), dma(4), dma(4), dma(3), dma(3), dma(8), dma(8),
            dma(3, 4), dma(3, 4), dma(2, 2), dma(2, 2), dma(2), dma(2), dma(3), dma(3), dma(2), dma(2), dma(6), dma(6),
            pltpu.SemaphoreType.DMA, pltpu.SemaphoreType.DMA, dma(4), dma(4), dma(3), dma(3), dma(2), dma(2),
            dma(3, 3), dma(3, 3),
        ],
        compiler_params=pltpu.CompilerParams(
            collective_id=0, has_side_effects=True, vmem_limit_bytes=62 * 2**20
        ),
        name="block",
    )(neighbors, queries, keys, values, w_out.T, grad_out)
    out, gq, gk, gv, gwt = pl.pallas_call(
        deliver,
        out_shape=(big, big, big, big, jax.ShapeDtypeStruct((PIECE, COLS), F32)),
        in_specs=[whole] * 5,
        out_specs=[whole] * 5,
        name="deliver",
    )(out, gq, gk, gv, gwt)
    return (out, gq, gk, gv, gwt.T)


def solution(mesh):
    placed = (
        P("sp", "fsdp"),
        P("sp", "fsdp"),
        P("sp", "fsdp"),
        P("fsdp", "sp"),
        P("sp", "fsdp"),
        P("sp", None),
    )
    return jax.shard_map(
        local,
        mesh=mesh,
        in_specs=placed,
        out_specs=(
            P("sp", "fsdp"),
            P("sp", "fsdp"),
            P("sp", "fsdp"),
            P("sp", "fsdp"),
            P("fsdp", "sp"),
        ),
        check_vma=False,
    )
```

```python
import math

import jax
import jax.numpy as jnp
from jax import lax
from jax.experimental import pallas as pl
from jax.experimental.pallas import tpu as pltpu
from jax.sharding import PartitionSpec as P

HD = 128
TILE = 384
HEADS = 3
TOK = 768
COLS = 384
WIN = 5 * TILE
WIDE = 6 * TILE
PIECE = 96
HALF = 48
MESH = pl.DeviceIdType.MESH
SCALE = 1.0 / math.sqrt(HD)
LOG2E = 1.4426950408889634
NEG_FILL = -1e30
BF = jnp.bfloat16
F32 = jnp.float32


def dot_nn(a, b):
    return lax.dot_general(a, b, (((1,), (0,)), ((), ())), preferred_element_type=F32)


def dot_nt(a, b):
    return lax.dot_general(a, b, (((1,), (1,)), ((), ())), preferred_element_type=F32)


def dot_tn(a, b):
    return lax.dot_general(a, b, (((0,), (0,)), ((), ())), preferred_element_type=F32)


def aligned(start, size):
    return pl.ds(pl.multiple_of(start, size), size)


def kernel(
    nb_ref, q_ref, k_ref, v_ref, w_ref, go_ref,
    out_ref, gq_ref, gk_ref, gv_ref, gw_ref,
    kw, vw, gall, wt, att, scores, probs, inv_total,
    gsend, grecv, gown, gatt,
    osend, orecv, oown, held,
    gw, cs, cr, rs_s, rs_r, ls_s, ls_r, ys, yr,
    dka, dva, hs, hr,
    local_sem, wy_s, wy_r, wr_s, wr_r, wl_s, wl_r, wc_s, wc_r,
    kv_s, kv_r, ga_s, ga_r, gf_s, gf_r, at_s, at_r, gr_s, gr_r, or_s, or_r,
    gc_s, gc_r, gright_s, gright_r, gleft_s, gleft_r, gy_s, gy_r, hk_s, hk_r,
):
    f = lax.axis_index("fsdp")
    s = lax.axis_index("sp")
    ylo, x = f // 4, f % 4
    yhi, z, core = s // 16, (s // 2) % 8, s % 2

    def device(ylo_at, x_at, yhi_at, z_at, core_at):
        return (ylo_at * 4 + x_at, yhi_at * 16 + z_at * 2 + core_at)

    z_next = device(ylo, x, yhi, (z + 1) % 8, core)
    z_prev = device(ylo, x, yhi, (z + 7) % 8, core)
    partner = device(ylo, x, yhi, z, 1 - core)
    y_partner = device(1 - ylo, x, yhi, z, core)
    sp_next = (f, (s + 1) % 32)
    sp_prev = (f, (s + 31) % 32)

    def x_at(k):
        return device(ylo, (x + k) % 4, yhi, z, core)

    def remote(src, dst, send, recv, to):
        return pltpu.make_async_remote_copy(
            src_ref=src, dst_ref=dst, send_sem=send, recv_sem=recv, device_id=to, device_id_type=MESH
        )

    barrier = pltpu.get_barrier_semaphore()
    greeted = [
        z_next, z_prev, partner, sp_next, sp_prev, y_partner,
        device(ylo, x, 1 - yhi, z, core), device(1 - ylo, x, 1 - yhi, z, core),
        x_at(1), x_at(2), x_at(3),
    ]
    for other in greeted:
        pl.semaphore_signal(barrier, inc=1, device_id=other, device_id_type=MESH)
    pl.semaphore_wait(barrier, len(greeted))

    def slot(z_at, core_at):
        return pl.ds(pl.multiple_of((z_at * 2 + core_at) * PIECE, 32), PIECE)

    w_lanes = aligned(ylo * COLS, 128 * 3)

    def w_out_copy(k):
        return remote(
            w_ref, wt.at[slot(z, core), w_lanes], wy_s.at[k], wy_r.at[ylo], device(yhi, x, k, z, core)
        )

    def w_self_copy():
        return pltpu.make_async_copy(w_ref, wt.at[slot(z, core), w_lanes], local_sem.at[0])

    same = ylo == yhi
    for k in range(2):
        to_self = jnp.logical_and(same, yhi == k)

        @pl.when(jnp.logical_not(to_self))
        def _():
            w_out_copy(k).start()

    @pl.when(same)
    def _():
        w_self_copy().start()

    def lanes(h):
        return aligned(h * HD, HD)

    def kv_copies(h):
        made = []
        for i, (src, dst) in enumerate(((k_ref, kw), (v_ref, vw))):
            made.append(remote(
                src.at[:, lanes(h)], dst.at[pl.ds(0, TOK), lanes(h)],
                kv_s.at[h, 2 * i], kv_r.at[h, 2 * i], sp_next))
            made.append(remote(
                src.at[:, lanes(h)], dst.at[pl.ds(2 * TOK, TOK), lanes(h)],
                kv_s.at[h, 2 * i + 1], kv_r.at[h, 2 * i + 1], sp_prev))
        return made

    has_prev, has_next = s > 0, s < 31

    def kv_start(h):
        copies = kv_copies(h)

        @pl.when(has_next)
        def _():
            copies[0].start()
            copies[2].start()

        @pl.when(has_prev)
        def _():
            copies[1].start()
            copies[3].start()

    def kv_wait(h):
        copies = kv_copies(h)

        @pl.when(has_prev)
        def _():
            copies[0].wait_recv()
            copies[2].wait_recv()

        @pl.when(has_next)
        def _():
            copies[1].wait_recv()
            copies[3].wait_recv()

    kv_start(0)

    def go_copy(t, left):
        rows = pl.ds(t * TILE, TILE)
        return remote(
            go_ref.at[rows, :], gall.at[rows, aligned(x * COLS, COLS)],
            ga_s.at[left, t], ga_r.at[left, t], x_at(3 if left else 1))

    def go_relay(left):
        at = gall.at[pl.ds(left * TILE, TILE), aligned((x + (1 if left else 3)) % 4 * COLS, COLS)]
        return remote(at, at, gf_s.at[left], gf_r.at[left], x_at(3 if left else 1))

    go_copy(0, 0).start()
    go_copy(1, 1).start()
    go_copy(1, 0).start()
    go_copy(0, 1).start()

    own = pl.ds(TOK, TOK)
    for side, missing in ((0, s == 0), (1, s == 31)):
        @pl.when(missing)
        def _():
            outside = pl.ds(side * 2 * TOK, TOK)
            kw[outside, :] = jnp.zeros((TOK, COLS), BF)
            vw[outside, :] = jnp.zeros((TOK, COLS), BF)
            hr[1 - side] = jnp.zeros((2, TOK, COLS), BF)

    locals_in = [
        pltpu.make_async_copy(k_ref, kw.at[own, :], local_sem.at[1]),
        pltpu.make_async_copy(v_ref, vw.at[own, :], local_sem.at[2]),
        pltpu.make_async_copy(go_ref, gall.at[:, aligned(x * COLS, COLS)], local_sem.at[3]),
    ]
    for copy in locals_in:
        copy.start()
    for copy in locals_in:
        copy.wait()

    def w_rows(z_at, i, half):
        start = (z_at * 2 + core) * PIECE
        if i < 3:
            return pl.ds(pl.multiple_of(start, 32), PIECE)
        return pl.ds(pl.multiple_of(start + half * HALF, 16), HALF)

    def w_right(i):
        at = wt.at[w_rows((z + 8 - i) % 8, i, 0), :]
        return remote(at, at, wr_s.at[i], wr_r.at[i], z_next)

    def w_left(i):
        at = wt.at[w_rows((z + i) % 8, i, 1), :]
        return remote(at, at, wl_s.at[i], wl_r.at[i], z_prev)

    def w_core(i, z_at):
        at = wt.at[slot(z_at, core), :]
        return remote(at, at, wc_s.at[i], wc_r.at[i], partner)

    def w_ring_start():
        @pl.when(same)
        def _():
            w_self_copy().wait()

        for i in range(2):
            from_self = jnp.logical_and(same, ylo == i)

            @pl.when(jnp.logical_not(from_self))
            def _():
                remote(
                    w_ref, wt.at[slot(z, core), pl.ds(i * COLS, COLS)], wy_s.at[0], wy_r.at[i], partner
                ).wait_recv()

        w_right(0).start()
        w_left(0).start()
        w_core(0, z).start()

    def w_ring_step(i):
        w_right(i - 1).wait_recv()
        if i < 4:
            w_right(i).start()
            w_core(i, (z + 8 - i) % 8).start()
        w_left(i - 1).wait_recv()
        if i < 4:
            w_left(i).start()
        w_core(4 + i if i < 4 else 4, (z + i) % 8).start()

    w_ring_start()
    kv_start(1)

    first = s * 2 - 2

    def forward(h, t):
        rows = aligned(t * TILE, TILE)
        query = q_ref[rows, lanes(h)]
        top = jnp.full((1, TILE), -3e38, F32)
        for j in range(5):
            tile_id = first + t + j
            hit = nb_ref[t, 0] == tile_id
            for i in range(1, 5):
                hit = jnp.logical_or(hit, nb_ref[t, i] == tile_id)
            hit = jnp.logical_and(hit, tile_id >= 0)
            bias = jnp.where(hit, 0.0, NEG_FILL)
            key = kw[aligned((t + j) * TILE, TILE), lanes(h)]
            block = dot_nt(key, query) * (SCALE * LOG2E) + bias
            scores[pl.ds(j * TILE, TILE), :] = block
            top = jnp.maximum(top, jnp.max(block, axis=0, keepdims=True))
        total = jnp.zeros((1, TILE), F32)
        u = h * 2 + t
        for j in range(5):
            e = jnp.exp2(scores[pl.ds(j * TILE, TILE), :] - top)
            total = total + jnp.sum(e, axis=0, keepdims=True)
            probs[u, pl.ds(j * TILE, TILE), :] = e.astype(BF)
        turned = dot_tn(
            vw[pl.ds(pl.multiple_of(t * TILE, TILE), WIN), lanes(h)], probs[u]
        )
        inv = 1.0 / total
        inv_total[u] = inv
        att[rows, pl.ds(pl.multiple_of(ylo * COLS + h * HD, HD), HD)] = (turned * inv).T.astype(BF)

    def att_copy(h):
        at = att.at[:, pl.ds(pl.multiple_of(ylo * COLS + h * HD, HD), HD)]
        return remote(at, at, at_s.at[h], at_r.at[h], y_partner)

    def fwd_step(u, carry):
        h, t = u // 2, u % 2

        @pl.when(t == 0)
        def _():
            kv_wait(h)

        @pl.when(u == 1)
        def _():
            w_ring_step(1)
            kv_start(2)

        @pl.when(u == 2)
        def _():
            go_copy(0, 0).wait_recv()
            go_relay(0).start()
            go_copy(1, 1).wait_recv()
            go_relay(1).start()

        for i in range(2, 4):
            @pl.when(u == 2 * i - 1)
            def _():
                w_ring_step(i)

        forward(h, t)

        @pl.when(t == 1)
        def _():
            att_copy(h).start()

        return carry

    lax.fori_loop(0, 2 * HEADS, fwd_step, 0)
    go_copy(1, 0).wait_recv()
    go_copy(0, 1).wait_recv()
    go_relay(0).wait_recv()
    go_relay(1).wait_recv()

    def gw_half(half):
        at = aligned(half * COLS, COLS)

        def gw_step(i, carry):
            part = dot_tn(gall[:, aligned(i * COLS, COLS)], att[:, at])
            gw[pl.ds(i * 4, 4), :, at] = part.reshape(4, PIECE, COLS)
            return carry

        lax.fori_loop(0, 4, gw_step, 0)

    gw_half(ylo)
    w_ring_step(4)
    for i in range(8):
        w_core(i, z).wait_recv()

    def gr_copy(t):
        rows = aligned(t * TILE, TILE)
        return remote(gsend.at[rows, :], grecv.at[rows, :], gr_s.at[t], gr_r.at[t], y_partner)

    def grad_step(t, carry):
        rows = aligned(t * TILE, TILE)
        block = gall[rows, :]
        gsend[rows, :] = dot_nn(block, wt[:, aligned((1 - ylo) * COLS, COLS)]).astype(BF)
        gr_copy(t).start()
        gown[rows, :] = dot_nn(block, wt[:, aligned(ylo * COLS, COLS)])
        return carry

    lax.fori_loop(0, 2, grad_step, 0)
    for h in range(HEADS):
        att_copy(h).wait_recv()
    gw_half(1 - ylo)

    def gw_cast(i, carry):
        cs[i] = gw[i * 2 + 1 - core].astype(BF)
        return carry

    lax.fori_loop(0, 8, gw_cast, 0)
    core_copy = remote(cs, cr, gc_s, gc_r, partner)
    core_copy.start()
    def g_copy(i, left):
        sent, landed = (ls_s, ls_r) if left else (rs_s, rs_r)
        send, recv = (gleft_s, gleft_r) if left else (gright_s, gright_r)
        at = (i, pl.ds(left * HALF, HALF)) if i == 0 else (i,)
        return remote(sent.at[at], landed.at[at], send.at[i], recv.at[i], z_prev if left else z_next)

    def chip_sum(z_at):
        return gw[z_at * 2 + core] + cr[z_at].astype(F32)

    def g_ring_step(i):
        if i == 0:
            core_copy.wait_recv()
        for left in range(2):
            sent, landed = (ls_s, ls_r) if left else (rs_s, rs_r)
            half = pl.ds(left * HALF, HALF)
            if i > 0:
                g_copy(i - 1, left).wait_recv()
            if i < 4:
                mine = chip_sum((z + 4 + i if left else z + 4 - i) % 8)
                if i > 1:
                    mine = mine + landed[i - 1].astype(F32)
                sent[i] = mine.astype(BF)
                if i == 1:
                    sent[1, half] = (mine[left * HALF:(left + 1) * HALF] + landed[0, half].astype(F32)).astype(BF)
                g_copy(i, left).start()

    def out_copy(i):
        return remote(osend.at[i], orecv.at[i], or_s.at[i], or_r.at[i], x_at(1 if i < 3 else 3))

    def out_part(k):
        return dot_nt(att[...], wt[aligned((x + k) % 4 * COLS, COLS), :])

    def out_send(i, part):
        osend[i] = part.astype(BF)
        out_copy(i).start()

    part = out_part(2)
    out_send(0, part[:TILE])
    out_send(3, part[TILE:])
    part = out_part(3)
    out_send(5, part[:TILE])
    held[1] = part[TILE:]
    g_ring_step(0)
    part = out_part(1)
    out_send(2, part[TILE:])
    held[0] = part[:TILE]
    oown[...] = out_part(0)

    def out_relay():
        for i in range(2):
            out_copy(3 * i).wait_recv()
            out_send(3 * i + 1, held[i] + orecv[3 * i].astype(F32))


    def halo_copy(h, i):
        side, rows = ((0, pl.ds(0, TILE)), (0, pl.ds(TILE, TILE)), (1, pl.ds(0, TOK)))[i]
        return remote(
            hs.at[side, :, rows, lanes(h)], hr.at[side, :, rows, lanes(h)], hk_s.at[h, i], hk_r.at[h, i],
            sp_next if side else sp_prev)

    def halo_send(h, i):
        side, first_row, count = ((0, 0, TILE), (0, TILE, TILE), (1, 0, TOK))[i]
        to = pl.ds(first_row, count)
        at = pl.ds(side * 2 * TOK + first_row, count)

        @pl.when(has_next if side else has_prev)
        def _():
            hs[side, 0, to, lanes(h)] = dka[at, lanes(h)].astype(BF)
            hs[side, 1, to, lanes(h)] = dva[at, lanes(h)].astype(BF)
            halo_copy(h, i).start()

    def backward(h, t):
        rows = pl.ds(t * TILE, TILE)
        u = h * 2 + t
        query = q_ref[rows, lanes(h)]
        grad = gatt[rows, lanes(h)]
        made = att[rows, pl.ds(pl.multiple_of(ylo * COLS + h * HD, HD), HD)]
        delta = jnp.sum((grad.astype(F32) * made.astype(F32)).T, axis=0, keepdims=True)
        inv = inv_total[u]
        factor = inv * SCALE
        shift = delta * factor
        inv_rows = jnp.broadcast_to(inv, (HD, TILE)).T
        grad_scaled = (grad.astype(F32) * inv_rows).astype(BF)
        turned = jnp.zeros((HD, TILE), F32)
        for j in ((0, 1, 2, 3, 4), (0, 3, 4, 1, 2))[t]:
            at = pl.ds((t + j) * TILE, TILE)
            key = kw[at, lanes(h)]
            value = vw[at, lanes(h)]
            prob = probs[u, pl.ds(j * TILE, TILE), :]
            inner = dot_nt(value, grad)
            ds = (prob.astype(F32) * (inner * factor - shift)).astype(BF)
            dk = dot_nn(ds, query)
            dv = dot_nn(prob, grad_scaled)
            if t == 0 or j == 4:
                dka[at, lanes(h)] = dk
                dva[at, lanes(h)] = dv
            else:
                dka[at, lanes(h)] += dk
                dva[at, lanes(h)] += dv
            turned = turned + dot_tn(key, ds)
            if t == 0 and j == 0:
                halo_send(h, 0)
            if t == 1 and j == 4:
                halo_send(h, 1)
                halo_send(h, 2)
        gq_ref[rows, lanes(h)] = turned.T.astype(BF)

    def gy_copy(i):
        return remote(ys.at[i], yr.at[yhi], gy_s.at[i], gy_r.at[yhi], device(i, x, ylo, z, core))

    def gy_self():
        return pltpu.make_async_copy(ys.at[ylo], yr.at[yhi], local_sem.at[4])

    def gy_start():
        z_sum = chip_sum(z) + rs_r[3].astype(F32) + ls_r[3].astype(F32)
        ys[0] = z_sum[:, :COLS]
        ys[1] = z_sum[:, COLS:]
        for i in range(2):
            to_self = jnp.logical_and(same, ylo == i)

            @pl.when(jnp.logical_not(to_self))
            def _():
                gy_copy(i).start()

        @pl.when(same)
        def _():
            gy_self().start()

    def grad_ready(t):
        gr_copy(t).wait_recv()
        rows = pl.ds(t * TILE, TILE)
        gatt[rows, :] = (gown[rows, :] + grecv[rows, :].astype(F32)).astype(BF)

    def bwd_step(i, carry):
        h = jnp.where(i < 4, i % 2, 2)
        t = jnp.where(i < 4, i // 2, i - 4)

        @pl.when(i == 0)
        def _():
            grad_ready(0)

        @pl.when(i == 1)
        def _():
            g_ring_step(1)

        @pl.when(i == 2)
        def _():
            grad_ready(1)
            out_relay()
            g_ring_step(2)

        @pl.when(i == 3)
        def _():
            g_ring_step(3)

        @pl.when(t == 0)
        def _():
            backward(h, 0)

        @pl.when(t == 1)
        def _():
            backward(h, 1)

        return carry

    lax.fori_loop(0, 2 * HEADS, bwd_step, 0)

    g_ring_step(4)
    gy_start()

    for i in (1, 2, 4, 5):
        out_copy(i).wait_recv()
    for t, i, j in ((0, 1, 5), (1, 4, 2)):
        rows = pl.ds(t * TILE, TILE)
        out_ref[rows, :] = (oown[rows, :] + orecv[i].astype(F32) + orecv[j].astype(F32)).astype(BF)

    for h in range(HEADS):
        @pl.when(has_next)
        def _():
            halo_copy(h, 0).wait_recv()
            halo_copy(h, 1).wait_recv()

        @pl.when(has_prev)
        def _():
            halo_copy(h, 2).wait_recv()

        at = pl.ds(h * HD, HD)
        gk_ref[:, at] = (
            dka[own, at] + hr[0, 0, :, at].astype(F32) + hr[1, 0, :, at].astype(F32)
        ).astype(BF)
        gv_ref[:, at] = (
            dva[own, at] + hr[0, 1, :, at].astype(F32) + hr[1, 1, :, at].astype(F32)
        ).astype(BF)

    @pl.when(same)
    def _():
        gy_self().wait()

    for i in range(2):
        from_self = jnp.logical_and(same, yhi == i)

        @pl.when(jnp.logical_not(from_self))
        def _():
            remote(ys.at[i], yr.at[i], gy_s.at[i], gy_r.at[i], partner).wait_recv()

    gw_ref[...] = yr[0] + yr[1]

    for k in range(2):
        to_self = jnp.logical_and(same, yhi == k)

        @pl.when(jnp.logical_not(to_self))
        def _():
            w_out_copy(k).wait_send()

    for i in range(2):
        to_self = jnp.logical_and(same, ylo == i)

        @pl.when(jnp.logical_not(to_self))
        def _():
            gy_copy(i).wait_send()

    for h in range(HEADS):
        copies = kv_copies(h)

        @pl.when(has_next)
        def _():
            for copy in (copies[0], copies[2], halo_copy(h, 2)):
                copy.wait_send()

        @pl.when(has_prev)
        def _():
            for copy in (copies[1], copies[3], halo_copy(h, 0), halo_copy(h, 1)):
                copy.wait_send()

        att_copy(h).wait_send()
    for t in range(2):
        gr_copy(t).wait_send()
        go_copy(t, 0).wait_send()
        go_copy(t, 1).wait_send()
        go_relay(t).wait_send()
    for i in range(6):
        out_copy(i).wait_send()
    for i in range(4):
        w_right(i).wait_send()
        w_left(i).wait_send()
        g_copy(i, 0).wait_send()
        g_copy(i, 1).wait_send()
    for i in range(8):
        w_core(i, z).wait_send()
    core_copy.wait_send()


def deliver(*refs):
    for source, target in zip(refs[:5], refs[5:]):
        target[...] = source[...]


def local(queries, keys, values, w_out, grad_out, neighbors):
    vmem = lambda shape, dtype: pltpu.VMEM(shape, dtype)
    dma = lambda *shape: pltpu.SemaphoreType.DMA(shape)
    big = jax.ShapeDtypeStruct((TOK, COLS), BF)
    anywhere = pl.BlockSpec(memory_space=pl.ANY)
    whole = pl.BlockSpec(memory_space=pltpu.VMEM)
    out, gq, gk, gv, gwt = pl.pallas_call(
        kernel,
        out_shape=(big, big, big, big, jax.ShapeDtypeStruct((PIECE, COLS), F32)),
        in_specs=[pl.BlockSpec(memory_space=pltpu.SMEM), whole, anywhere, anywhere, anywhere, anywhere],
        out_specs=[whole] * 5,
        scratch_shapes=[
            vmem((WIDE, COLS), BF), vmem((WIDE, COLS), BF),
            vmem((TOK, 4 * COLS), BF), vmem((4 * COLS, 2 * COLS), BF), vmem((TOK, 2 * COLS), BF),
            vmem((WIN, TILE), F32), vmem((2 * HEADS, WIN, TILE), BF), vmem((2 * HEADS, 1, TILE), F32),
            vmem((TOK, COLS), BF), vmem((TOK, COLS), BF), vmem((TOK, COLS), F32), vmem((TOK, COLS), BF),
            vmem((6, TILE, COLS), BF), vmem((6, TILE, COLS), BF), vmem((TOK, COLS), F32), vmem((2, TILE, COLS), F32),
            vmem((16, PIECE, 2 * COLS), F32),
            vmem((8, PIECE, 2 * COLS), BF), vmem((8, PIECE, 2 * COLS), BF),
            vmem((4, PIECE, 2 * COLS), BF), vmem((4, PIECE, 2 * COLS), BF),
            vmem((4, PIECE, 2 * COLS), BF), vmem((4, PIECE, 2 * COLS), BF),
            vmem((2, PIECE, COLS), F32), vmem((2, PIECE, COLS), F32),
            vmem((WIDE, COLS), F32), vmem((WIDE, COLS), F32),
            vmem((2, 2, TOK, COLS), BF), vmem((2, 2, TOK, COLS), BF),
            dma(5), dma(2), dma(2), dma(4), dma(4), dma(4), dma(4), dma(8), dma(8),
            dma(3, 4), dma(3, 4), dma(2, 2), dma(2, 2), dma(2), dma(2), dma(3), dma(3), dma(2), dma(2), dma(6), dma(6),
            pltpu.SemaphoreType.DMA, pltpu.SemaphoreType.DMA, dma(4), dma(4), dma(4), dma(4), dma(2), dma(2),
            dma(3, 3), dma(3, 3),
        ],
        compiler_params=pltpu.CompilerParams(
            collective_id=0, has_side_effects=True, vmem_limit_bytes=62 * 2**20
        ),
        name="block",
    )(neighbors, queries, keys, values, w_out.T, grad_out)
    out, gq, gk, gv, gwt = pl.pallas_call(
        deliver,
        out_shape=(big, big, big, big, jax.ShapeDtypeStruct((PIECE, COLS), F32)),
        in_specs=[whole] * 5,
        out_specs=[whole] * 5,
        name="deliver",
    )(out, gq, gk, gv, gwt)
    return (out, gq, gk, gv, gwt.T)


def solution(mesh):
    placed = (
        P("sp", "fsdp"),
        P("sp", "fsdp"),
        P("sp", "fsdp"),
        P("fsdp", "sp"),
        P("sp", "fsdp"),
        P("sp", None),
    )
    return jax.shard_map(
        local,
        mesh=mesh,
        in_specs=placed,
        out_specs=(
            P("sp", "fsdp"),
            P("sp", "fsdp"),
            P("sp", "fsdp"),
            P("sp", "fsdp"),
            P("fsdp", "sp"),
        ),
        check_vma=False,
    )
```

```python
import math

import jax
import jax.numpy as jnp
from jax import lax
from jax.experimental import pallas as pl
from jax.experimental.pallas import tpu as pltpu
from jax.sharding import PartitionSpec as P

HD = 128
TILE = 384
HEADS = 3
TOK = 768
COLS = 384
WIN = 5 * TILE
WIDE = 6 * TILE
PIECE = 96
HALF = 48
MESH = pl.DeviceIdType.MESH
SCALE = 1.0 / math.sqrt(HD)
LOG2E = 1.4426950408889634
NEG_FILL = -1e30
BF = jnp.bfloat16
F32 = jnp.float32


def dot_nn(a, b):
    return lax.dot_general(a, b, (((1,), (0,)), ((), ())), preferred_element_type=F32)


def dot_nt(a, b):
    return lax.dot_general(a, b, (((1,), (1,)), ((), ())), preferred_element_type=F32)


def dot_tn(a, b):
    return lax.dot_general(a, b, (((0,), (0,)), ((), ())), preferred_element_type=F32)


def aligned(start, size):
    return pl.ds(pl.multiple_of(start, size), size)


def kernel(
    nb_ref, q_ref, k_ref, v_ref, w_ref, go_ref,
    out_ref, gq_ref, gk_ref, gv_ref, gw_ref,
    kw, vw, gall, wt, att, scores, probs, inv_total,
    gsend, grecv, gown, gatt,
    osend, orecv, oown, held,
    gw, cs, cr, rs_s, rs_r, ls_s, ls_r, ys, yr,
    dka, dva, hs, hr,
    local_sem, wy_s, wy_r, wr_s, wr_r, wl_s, wl_r, wc_s, wc_r,
    kv_s, kv_r, ga_s, ga_r, gf_s, gf_r, at_s, at_r, gr_s, gr_r, or_s, or_r,
    gc_s, gc_r, gright_s, gright_r, gleft_s, gleft_r, gy_s, gy_r, hk_s, hk_r,
):
    f = lax.axis_index("fsdp")
    s = lax.axis_index("sp")
    ylo, x = f // 4, f % 4
    yhi, z, core = s // 16, (s // 2) % 8, s % 2

    def device(ylo_at, x_at, yhi_at, z_at, core_at):
        return (ylo_at * 4 + x_at, yhi_at * 16 + z_at * 2 + core_at)

    z_next = device(ylo, x, yhi, (z + 1) % 8, core)
    z_prev = device(ylo, x, yhi, (z + 7) % 8, core)
    partner = device(ylo, x, yhi, z, 1 - core)
    y_partner = device(1 - ylo, x, yhi, z, core)
    sp_next = (f, (s + 1) % 32)
    sp_prev = (f, (s + 31) % 32)

    def x_at(k):
        return device(ylo, (x + k) % 4, yhi, z, core)

    def remote(src, dst, send, recv, to):
        return pltpu.make_async_remote_copy(
            src_ref=src, dst_ref=dst, send_sem=send, recv_sem=recv, device_id=to, device_id_type=MESH
        )

    barrier = pltpu.get_barrier_semaphore()
    greeted = [
        z_next, z_prev, partner, sp_next, sp_prev, y_partner,
        device(ylo, x, 1 - yhi, z, core), device(1 - ylo, x, 1 - yhi, z, core),
        x_at(1), x_at(2), x_at(3),
    ]
    for other in greeted:
        pl.semaphore_signal(barrier, inc=1, device_id=other, device_id_type=MESH)
    pl.semaphore_wait(barrier, len(greeted))

    def slot(z_at, core_at):
        return pl.ds(pl.multiple_of((z_at * 2 + core_at) * PIECE, 32), PIECE)

    w_lanes = aligned(ylo * COLS, 128 * 3)

    def w_out_copy(k):
        return remote(
            w_ref, wt.at[slot(z, core), w_lanes], wy_s.at[k], wy_r.at[ylo], device(yhi, x, k, z, core)
        )

    def w_self_copy():
        return pltpu.make_async_copy(w_ref, wt.at[slot(z, core), w_lanes], local_sem.at[0])

    same = ylo == yhi
    for k in range(2):
        to_self = jnp.logical_and(same, yhi == k)

        @pl.when(jnp.logical_not(to_self))
        def _():
            w_out_copy(k).start()

    @pl.when(same)
    def _():
        w_self_copy().start()

    def lanes(h):
        return aligned(h * HD, HD)

    def kv_copies(h):
        made = []
        for i, (src, dst) in enumerate(((k_ref, kw), (v_ref, vw))):
            made.append(remote(
                src.at[:, lanes(h)], dst.at[pl.ds(0, TOK), lanes(h)],
                kv_s.at[h, 2 * i], kv_r.at[h, 2 * i], sp_next))
            made.append(remote(
                src.at[:, lanes(h)], dst.at[pl.ds(2 * TOK, TOK), lanes(h)],
                kv_s.at[h, 2 * i + 1], kv_r.at[h, 2 * i + 1], sp_prev))
        return made

    has_prev, has_next = s > 0, s < 31

    def kv_start(h):
        copies = kv_copies(h)

        @pl.when(has_next)
        def _():
            copies[0].start()
            copies[2].start()

        @pl.when(has_prev)
        def _():
            copies[1].start()
            copies[3].start()

    def kv_wait(h):
        copies = kv_copies(h)

        @pl.when(has_prev)
        def _():
            copies[0].wait_recv()
            copies[2].wait_recv()

        @pl.when(has_next)
        def _():
            copies[1].wait_recv()
            copies[3].wait_recv()

    kv_start(0)

    def go_copy(t, left):
        rows = pl.ds(t * TILE, TILE)
        return remote(
            go_ref.at[rows, :], gall.at[rows, aligned(x * COLS, COLS)],
            ga_s.at[left, t], ga_r.at[left, t], x_at(3 if left else 1))

    def go_relay(left):
        at = gall.at[pl.ds(left * TILE, TILE), aligned((x + (1 if left else 3)) % 4 * COLS, COLS)]
        return remote(at, at, gf_s.at[left], gf_r.at[left], x_at(3 if left else 1))

    go_copy(0, 0).start()
    go_copy(1, 1).start()
    go_copy(1, 0).start()
    go_copy(0, 1).start()

    own = pl.ds(TOK, TOK)
    for side, missing in ((0, s == 0), (1, s == 31)):
        @pl.when(missing)
        def _():
            outside = pl.ds(side * 2 * TOK, TOK)
            kw[outside, :] = jnp.zeros((TOK, COLS), BF)
            vw[outside, :] = jnp.zeros((TOK, COLS), BF)
            hr[1 - side] = jnp.zeros((2, TOK, COLS), BF)

    locals_in = [
        pltpu.make_async_copy(k_ref, kw.at[own, :], local_sem.at[1]),
        pltpu.make_async_copy(v_ref, vw.at[own, :], local_sem.at[2]),
        pltpu.make_async_copy(go_ref, gall.at[:, aligned(x * COLS, COLS)], local_sem.at[3]),
    ]
    for copy in locals_in:
        copy.start()
    for copy in locals_in:
        copy.wait()

    def w_rows(z_at, i, half):
        start = (z_at * 2 + core) * PIECE
        if i < 3:
            return pl.ds(pl.multiple_of(start, 32), PIECE)
        return pl.ds(pl.multiple_of(start + half * HALF, 16), HALF)

    def w_right(i):
        at = wt.at[w_rows((z + 8 - i) % 8, i, 0), :]
        return remote(at, at, wr_s.at[i], wr_r.at[i], z_next)

    def w_left(i):
        at = wt.at[w_rows((z + i) % 8, i, 1), :]
        return remote(at, at, wl_s.at[i], wl_r.at[i], z_prev)

    def w_core(i, z_at):
        at = wt.at[slot(z_at, core), :]
        return remote(at, at, wc_s.at[i], wc_r.at[i], partner)

    def w_ring_start():
        @pl.when(same)
        def _():
            w_self_copy().wait()

        for i in range(2):
            from_self = jnp.logical_and(same, ylo == i)

            @pl.when(jnp.logical_not(from_self))
            def _():
                remote(
                    w_ref, wt.at[slot(z, core), pl.ds(i * COLS, COLS)], wy_s.at[0], wy_r.at[i], partner
                ).wait_recv()

        w_right(0).start()
        w_left(0).start()
        w_core(0, z).start()

    def w_ring_step(i):
        w_right(i - 1).wait_recv()
        if i < 4:
            w_right(i).start()
            w_core(i, (z + 8 - i) % 8).start()
        w_left(i - 1).wait_recv()
        if i < 4:
            w_left(i).start()
        w_core(4 + i if i < 4 else 4, (z + i) % 8).start()

    w_ring_start()
    kv_start(1)

    first = s * 2 - 2

    def forward(h, t):
        rows = aligned(t * TILE, TILE)
        query = q_ref[rows, lanes(h)]
        top = jnp.full((1, TILE), -3e38, F32)
        for j in range(5):
            tile_id = first + t + j
            hit = nb_ref[t, 0] == tile_id
            for i in range(1, 5):
                hit = jnp.logical_or(hit, nb_ref[t, i] == tile_id)
            hit = jnp.logical_and(hit, tile_id >= 0)
            bias = jnp.where(hit, 0.0, NEG_FILL)
            key = kw[aligned((t + j) * TILE, TILE), lanes(h)]
            block = dot_nt(key, query) * (SCALE * LOG2E) + bias
            scores[pl.ds(j * TILE, TILE), :] = block
            top = jnp.maximum(top, jnp.max(block, axis=0, keepdims=True))
        total = jnp.zeros((1, TILE), F32)
        u = h * 2 + t
        for j in range(5):
            e = jnp.exp2(scores[pl.ds(j * TILE, TILE), :] - top)
            total = total + jnp.sum(e, axis=0, keepdims=True)
            probs[u, pl.ds(j * TILE, TILE), :] = e.astype(BF)
        turned = dot_tn(
            vw[pl.ds(pl.multiple_of(t * TILE, TILE), WIN), lanes(h)], probs[u]
        )
        inv = 1.0 / total
        inv_total[u] = inv
        att[rows, pl.ds(pl.multiple_of(ylo * COLS + h * HD, HD), HD)] = (turned * inv).T.astype(BF)

    def att_copy(h):
        at = att.at[:, pl.ds(pl.multiple_of(ylo * COLS + h * HD, HD), HD)]
        return remote(at, at, at_s.at[h], at_r.at[h], y_partner)

    def fwd_step(u, carry):
        h, t = u // 2, u % 2

        @pl.when(t == 0)
        def _():
            kv_wait(h)

        @pl.when(u == 1)
        def _():
            w_ring_step(1)
            kv_start(2)

        @pl.when(u == 2)
        def _():
            go_copy(0, 0).wait_recv()
            go_relay(0).start()
            go_copy(1, 1).wait_recv()
            go_relay(1).start()

        for i in range(2, 4):
            @pl.when(u == 2 * i - 1)
            def _():
                w_ring_step(i)

        forward(h, t)

        @pl.when(t == 1)
        def _():
            att_copy(h).start()

        return carry

    lax.fori_loop(0, 2 * HEADS, fwd_step, 0)
    go_copy(1, 0).wait_recv()
    go_copy(0, 1).wait_recv()
    go_relay(0).wait_recv()
    go_relay(1).wait_recv()

    def gw_half(half):
        at = aligned(half * COLS, COLS)

        def gw_step(i, carry):
            part = dot_tn(gall[:, aligned(i * COLS, COLS)], att[:, at])
            gw[pl.ds(i * 4, 4), :, at] = part.reshape(4, PIECE, COLS)
            return carry

        lax.fori_loop(0, 4, gw_step, 0)

    gw_half(ylo)
    w_ring_step(4)
    for i in range(8):
        w_core(i, z).wait_recv()

    def gr_copy(t):
        rows = aligned(t * TILE, TILE)
        return remote(gsend.at[rows, :], grecv.at[rows, :], gr_s.at[t], gr_r.at[t], y_partner)

    def grad_step(t, carry):
        rows = aligned(t * TILE, TILE)
        block = gall[rows, :]
        gsend[rows, :] = dot_nn(block, wt[:, aligned((1 - ylo) * COLS, COLS)]).astype(BF)
        gr_copy(t).start()
        gown[rows, :] = dot_nn(block, wt[:, aligned(ylo * COLS, COLS)])
        return carry

    lax.fori_loop(0, 2, grad_step, 0)
    for h in range(HEADS):
        att_copy(h).wait_recv()
    gw_half(1 - ylo)

    def gw_cast(i, carry):
        cs[i] = gw[i * 2 + 1 - core].astype(BF)
        return carry

    lax.fori_loop(0, 8, gw_cast, 0)
    core_copy = remote(cs, cr, gc_s, gc_r, partner)
    core_copy.start()
    def g_copy(i, left):
        sent, landed = (ls_s, ls_r) if left else (rs_s, rs_r)
        send, recv = (gleft_s, gleft_r) if left else (gright_s, gright_r)
        at = (i, pl.ds(left * HALF, HALF)) if i == 0 else (i,)
        return remote(sent.at[at], landed.at[at], send.at[i], recv.at[i], z_prev if left else z_next)

    def chip_sum(z_at):
        return gw[z_at * 2 + core] + cr[z_at].astype(F32)

    def g_ring_step(i):
        if i == 0:
            core_copy.wait_recv()
        for left in range(2):
            sent, landed = (ls_s, ls_r) if left else (rs_s, rs_r)
            half = pl.ds(left * HALF, HALF)
            if i > 0:
                g_copy(i - 1, left).wait_recv()
            if i < 4:
                mine = chip_sum((z + 4 + i if left else z + 4 - i) % 8)
                if i > 1:
                    mine = mine + landed[i - 1].astype(F32)
                sent[i] = mine.astype(BF)
                if i == 1:
                    sent[1, half] = (mine[left * HALF:(left + 1) * HALF] + landed[0, half].astype(F32)).astype(BF)
                g_copy(i, left).start()

    def out_copy(i):
        return remote(osend.at[i], orecv.at[i], or_s.at[i], or_r.at[i], x_at(1 if i < 3 else 3))

    def out_part(k):
        return dot_nt(att[...], wt[aligned((x + k) % 4 * COLS, COLS), :])

    def out_send(i, part):
        osend[i] = part.astype(BF)
        out_copy(i).start()

    part = out_part(2)
    out_send(0, part[:TILE])
    out_send(3, part[TILE:])
    part = out_part(3)
    out_send(5, part[:TILE])
    held[1] = part[TILE:]
    g_ring_step(0)
    part = out_part(1)
    out_send(2, part[TILE:])
    held[0] = part[:TILE]
    oown[...] = out_part(0)

    def out_relay():
        for i in range(2):
            out_copy(3 * i).wait_recv()
            out_send(3 * i + 1, held[i] + orecv[3 * i].astype(F32))


    def halo_copy(h, i):
        side, rows = ((0, pl.ds(0, TILE)), (0, pl.ds(TILE, TILE)), (1, pl.ds(0, TOK)))[i]
        return remote(
            hs.at[side, :, rows, lanes(h)], hr.at[side, :, rows, lanes(h)], hk_s.at[h, i], hk_r.at[h, i],
            sp_next if side else sp_prev)

    def halo_send(h, i):
        side, first_row, count = ((0, 0, TILE), (0, TILE, TILE), (1, 0, TOK))[i]
        to = pl.ds(first_row, count)
        at = pl.ds(side * 2 * TOK + first_row, count)

        @pl.when(has_next if side else has_prev)
        def _():
            hs[side, 0, to, lanes(h)] = dka[at, lanes(h)].astype(BF)
            hs[side, 1, to, lanes(h)] = dva[at, lanes(h)].astype(BF)
            halo_copy(h, i).start()

    def backward(h, t):
        rows = pl.ds(t * TILE, TILE)
        u = h * 2 + t
        query = q_ref[rows, lanes(h)]
        grad = gatt[rows, lanes(h)]
        made = att[rows, pl.ds(pl.multiple_of(ylo * COLS + h * HD, HD), HD)]
        delta = jnp.sum((grad.astype(F32) * made.astype(F32)).T, axis=0, keepdims=True)
        inv = inv_total[u]
        factor = inv * SCALE
        shift = delta * factor
        inv_rows = jnp.broadcast_to(inv, (HD, TILE)).T
        grad_scaled = (grad.astype(F32) * inv_rows).astype(BF)
        turned = jnp.zeros((HD, TILE), F32)
        for j in ((0, 1, 2, 3, 4), (0, 3, 4, 1, 2))[t]:
            at = pl.ds((t + j) * TILE, TILE)
            key = kw[at, lanes(h)]
            value = vw[at, lanes(h)]
            prob = probs[u, pl.ds(j * TILE, TILE), :]
            inner = dot_nt(value, grad)
            ds = (prob.astype(F32) * (inner * factor - shift)).astype(BF)
            dk = dot_nn(ds, query)
            dv = dot_nn(prob, grad_scaled)
            if t == 0 or j == 4:
                dka[at, lanes(h)] = dk
                dva[at, lanes(h)] = dv
            else:
                dka[at, lanes(h)] += dk
                dva[at, lanes(h)] += dv
            turned = turned + dot_tn(key, ds)
            if t == 0 and j == 0:
                halo_send(h, 0)
            if t == 1 and j == 4:
                halo_send(h, 1)
                halo_send(h, 2)
        gq_ref[rows, lanes(h)] = turned.T.astype(BF)

    def gy_copy(i):
        return remote(ys.at[i], yr.at[yhi], gy_s.at[i], gy_r.at[yhi], device(i, x, ylo, z, core))

    def gy_self():
        return pltpu.make_async_copy(ys.at[ylo], yr.at[yhi], local_sem.at[4])

    def gy_start():
        z_sum = chip_sum(z) + rs_r[3].astype(F32) + ls_r[3].astype(F32)
        ys[0] = z_sum[:, :COLS]
        ys[1] = z_sum[:, COLS:]
        for i in range(2):
            to_self = jnp.logical_and(same, ylo == i)

            @pl.when(jnp.logical_not(to_self))
            def _():
                gy_copy(i).start()

        @pl.when(same)
        def _():
            gy_self().start()

    def grad_ready(t):
        gr_copy(t).wait_recv()
        rows = pl.ds(t * TILE, TILE)
        gatt[rows, :] = (gown[rows, :] + grecv[rows, :].astype(F32)).astype(BF)

    def bwd_step(i, carry):
        h = jnp.where(i < 4, i % 2, 2)
        t = jnp.where(i < 4, i // 2, i - 4)

        @pl.when(i == 0)
        def _():
            grad_ready(0)

        @pl.when(i == 1)
        def _():
            g_ring_step(1)

        @pl.when(i == 2)
        def _():
            grad_ready(1)
            out_relay()
            g_ring_step(2)

        @pl.when(i == 3)
        def _():
            g_ring_step(3)

        @pl.when(t == 0)
        def _():
            backward(h, 0)

        @pl.when(t == 1)
        def _():
            backward(h, 1)

        return carry

    lax.fori_loop(0, 2 * HEADS, bwd_step, 0)

    g_ring_step(4)
    gy_start()

    for i in (1, 2, 4, 5):
        out_copy(i).wait_recv()
    for t, i, j in ((0, 1, 5), (1, 4, 2)):
        rows = pl.ds(t * TILE, TILE)
        out_ref[rows, :] = (oown[rows, :] + orecv[i].astype(F32) + orecv[j].astype(F32)).astype(BF)

    for h in range(HEADS):
        @pl.when(has_next)
        def _():
            halo_copy(h, 0).wait_recv()
            halo_copy(h, 1).wait_recv()

        @pl.when(has_prev)
        def _():
            halo_copy(h, 2).wait_recv()

        at = pl.ds(h * HD, HD)
        gk_ref[:, at] = (
            dka[own, at] + hr[0, 0, :, at].astype(F32) + hr[1, 0, :, at].astype(F32)
        ).astype(BF)
        gv_ref[:, at] = (
            dva[own, at] + hr[0, 1, :, at].astype(F32) + hr[1, 1, :, at].astype(F32)
        ).astype(BF)

    @pl.when(same)
    def _():
        gy_self().wait()

    for i in range(2):
        from_self = jnp.logical_and(same, yhi == i)

        @pl.when(jnp.logical_not(from_self))
        def _():
            remote(ys.at[i], yr.at[i], gy_s.at[i], gy_r.at[i], partner).wait_recv()

    gw_ref[...] = yr[0] + yr[1]

    for k in range(2):
        to_self = jnp.logical_and(same, yhi == k)

        @pl.when(jnp.logical_not(to_self))
        def _():
            w_out_copy(k).wait_send()

    for i in range(2):
        to_self = jnp.logical_and(same, ylo == i)

        @pl.when(jnp.logical_not(to_self))
        def _():
            gy_copy(i).wait_send()

    for h in range(HEADS):
        copies = kv_copies(h)

        @pl.when(has_next)
        def _():
            for copy in (copies[0], copies[2], halo_copy(h, 2)):
                copy.wait_send()

        @pl.when(has_prev)
        def _():
            for copy in (copies[1], copies[3], halo_copy(h, 0), halo_copy(h, 1)):
                copy.wait_send()

        att_copy(h).wait_send()
    for t in range(2):
        gr_copy(t).wait_send()
        go_copy(t, 0).wait_send()
        go_copy(t, 1).wait_send()
        go_relay(t).wait_send()
    for i in range(6):
        out_copy(i).wait_send()
    for i in range(4):
        w_right(i).wait_send()
        w_left(i).wait_send()
        g_copy(i, 0).wait_send()
        g_copy(i, 1).wait_send()
    for i in range(8):
        w_core(i, z).wait_send()
    core_copy.wait_send()


def deliver(*refs):
    for source, target in zip(refs[:5], refs[5:]):
        target[...] = source[...]


def local(queries, keys, values, w_out, grad_out, neighbors):
    vmem = lambda shape, dtype: pltpu.VMEM(shape, dtype)
    dma = lambda *shape: pltpu.SemaphoreType.DMA(shape)
    big = jax.ShapeDtypeStruct((TOK, COLS), BF)
    anywhere = pl.BlockSpec(memory_space=pl.ANY)
    whole = pl.BlockSpec(memory_space=pltpu.VMEM)
    out, gq, gk, gv, gwt = pl.pallas_call(
        kernel,
        out_shape=(big, big, big, big, jax.ShapeDtypeStruct((PIECE, COLS), F32)),
        in_specs=[pl.BlockSpec(memory_space=pltpu.SMEM), whole, anywhere, anywhere, anywhere, anywhere],
        out_specs=[whole] * 5,
        scratch_shapes=[
            vmem((WIDE, COLS), BF), vmem((WIDE, COLS), BF),
            vmem((TOK, 4 * COLS), BF), vmem((4 * COLS, 2 * COLS), BF), vmem((TOK, 2 * COLS), BF),
            vmem((WIN, TILE), F32), vmem((2 * HEADS, WIN, TILE), BF), vmem((2 * HEADS, 1, TILE), F32),
            vmem((TOK, COLS), BF), vmem((TOK, COLS), BF), vmem((TOK, COLS), F32), vmem((TOK, COLS), BF),
            vmem((6, TILE, COLS), BF), vmem((6, TILE, COLS), BF), vmem((TOK, COLS), F32), vmem((2, TILE, COLS), F32),
            vmem((16, PIECE, 2 * COLS), F32),
            vmem((8, PIECE, 2 * COLS), BF), vmem((8, PIECE, 2 * COLS), BF),
            vmem((4, PIECE, 2 * COLS), BF), vmem((4, PIECE, 2 * COLS), BF),
            vmem((4, PIECE, 2 * COLS), BF), vmem((4, PIECE, 2 * COLS), BF),
            vmem((2, PIECE, COLS), F32), vmem((2, PIECE, COLS), F32),
            vmem((WIDE, COLS), F32), vmem((WIDE, COLS), F32),
            vmem((2, 2, TOK, COLS), BF), vmem((2, 2, TOK, COLS), BF),
            dma(5), dma(2), dma(2), dma(4), dma(4), dma(4), dma(4), dma(8), dma(8),
            dma(3, 4), dma(3, 4), dma(2, 2), dma(2, 2), dma(2), dma(2), dma(3), dma(3), dma(2), dma(2), dma(6), dma(6),
            pltpu.SemaphoreType.DMA, pltpu.SemaphoreType.DMA, dma(4), dma(4), dma(4), dma(4), dma(2), dma(2),
            dma(3, 3), dma(3, 3),
        ],
        compiler_params=pltpu.CompilerParams(
            collective_id=0, has_side_effects=True, vmem_limit_bytes=62 * 2**20
        ),
        name="block",
    )(neighbors, queries, keys, values, w_out.T, grad_out)
    parts = [pl.BlockSpec((TOK // 3, COLS), lambda i: (i, 0))] * 4
    parts.append(pl.BlockSpec((PIECE // 3, COLS), lambda i: (i, 0)))
    out, gq, gk, gv, gwt = pl.pallas_call(
        deliver,
        out_shape=(big, big, big, big, jax.ShapeDtypeStruct((PIECE, COLS), F32)),
        grid=(3,),
        in_specs=parts,
        out_specs=parts,
        name="deliver",
    )(out, gq, gk, gv, gwt)
    return (out, gq, gk, gv, gwt.T)


def solution(mesh):
    placed = (
        P("sp", "fsdp"),
        P("sp", "fsdp"),
        P("sp", "fsdp"),
        P("fsdp", "sp"),
        P("sp", "fsdp"),
        P("sp", None),
    )
    return jax.shard_map(
        local,
        mesh=mesh,
        in_specs=placed,
        out_specs=(
            P("sp", "fsdp"),
            P("sp", "fsdp"),
            P("sp", "fsdp"),
            P("sp", "fsdp"),
            P("fsdp", "sp"),
        ),
        check_vma=False,
    )
```

```python
import math

import jax
import jax.numpy as jnp
from jax import lax
from jax.experimental import pallas as pl
from jax.experimental.pallas import tpu as pltpu
from jax.sharding import PartitionSpec as P

HD = 128
TILE = 384
HEADS = 3
TOK = 768
COLS = 384
WIN = 5 * TILE
WIDE = 6 * TILE
PIECE = 96
HALF = 48
MESH = pl.DeviceIdType.MESH
SCALE = 1.0 / math.sqrt(HD)
LOG2E = 1.4426950408889634
NEG_FILL = -1e30
BF = jnp.bfloat16
F32 = jnp.float32


def dot_nn(a, b):
    return lax.dot_general(a, b, (((1,), (0,)), ((), ())), preferred_element_type=F32)


def dot_nt(a, b):
    return lax.dot_general(a, b, (((1,), (1,)), ((), ())), preferred_element_type=F32)


def dot_tn(a, b):
    return lax.dot_general(a, b, (((0,), (0,)), ((), ())), preferred_element_type=F32)


def aligned(start, size):
    return pl.ds(pl.multiple_of(start, size), size)


def kernel(
    nb_ref, q_ref, k_ref, v_ref, w_ref, go_ref,
    out_ref, gq_ref, gk_ref, gv_ref, gw_ref,
    kw, vw, gall, wt, att, scores, probs, inv_total,
    gsend, grecv, gown, gatt,
    osend, orecv, oown, held,
    gw, cs, cr, rs_s, rs_r, ls_s, ls_r, ys, yr,
    dka, dva, hs, hr,
    local_sem, wy_s, wy_r, wr_s, wr_r, wl_s, wl_r, wc_s, wc_r,
    kv_s, kv_r, ga_s, ga_r, gf_s, gf_r, at_s, at_r, gr_s, gr_r, or_s, or_r,
    gc_s, gc_r, gright_s, gright_r, gleft_s, gleft_r, gy_s, gy_r, hk_s, hk_r,
):
    f = lax.axis_index("fsdp")
    s = lax.axis_index("sp")
    ylo, x = f // 4, f % 4
    yhi, z, core = s // 16, (s // 2) % 8, s % 2

    def device(ylo_at, x_at, yhi_at, z_at, core_at):
        return (ylo_at * 4 + x_at, yhi_at * 16 + z_at * 2 + core_at)

    z_next = device(ylo, x, yhi, (z + 1) % 8, core)
    z_prev = device(ylo, x, yhi, (z + 7) % 8, core)
    partner = device(ylo, x, yhi, z, 1 - core)
    y_partner = device(1 - ylo, x, yhi, z, core)
    sp_next = (f, (s + 1) % 32)
    sp_prev = (f, (s + 31) % 32)

    def x_at(k):
        return device(ylo, (x + k) % 4, yhi, z, core)

    def remote(src, dst, send, recv, to):
        return pltpu.make_async_remote_copy(
            src_ref=src, dst_ref=dst, send_sem=send, recv_sem=recv, device_id=to, device_id_type=MESH
        )

    barrier = pltpu.get_barrier_semaphore()
    greeted = [
        z_next, z_prev, partner, sp_next, sp_prev, y_partner,
        device(ylo, x, 1 - yhi, z, core), device(1 - ylo, x, 1 - yhi, z, core),
        x_at(1), x_at(2), x_at(3),
    ]
    for other in greeted:
        pl.semaphore_signal(barrier, inc=1, device_id=other, device_id_type=MESH)
    pl.semaphore_wait(barrier, len(greeted))

    def slot(z_at, core_at):
        return pl.ds(pl.multiple_of((z_at * 2 + core_at) * PIECE, 32), PIECE)

    w_lanes = aligned(ylo * COLS, 128 * 3)

    def w_out_copy(k):
        return remote(
            w_ref, wt.at[slot(z, core), w_lanes], wy_s.at[k], wy_r.at[ylo], device(yhi, x, k, z, core)
        )

    def w_self_copy():
        return pltpu.make_async_copy(w_ref, wt.at[slot(z, core), w_lanes], local_sem.at[0])

    same = ylo == yhi
    for k in range(2):
        to_self = jnp.logical_and(same, yhi == k)

        @pl.when(jnp.logical_not(to_self))
        def _():
            w_out_copy(k).start()

    @pl.when(same)
    def _():
        w_self_copy().start()

    def lanes(h):
        return aligned(h * HD, HD)

    def kv_copies(h):
        made = []
        for i, (src, dst) in enumerate(((k_ref, kw), (v_ref, vw))):
            made.append(remote(
                src.at[:, lanes(h)], dst.at[pl.ds(0, TOK), lanes(h)],
                kv_s.at[h, 2 * i], kv_r.at[h, 2 * i], sp_next))
            made.append(remote(
                src.at[:, lanes(h)], dst.at[pl.ds(2 * TOK, TOK), lanes(h)],
                kv_s.at[h, 2 * i + 1], kv_r.at[h, 2 * i + 1], sp_prev))
        return made

    has_prev, has_next = s > 0, s < 31

    def kv_start(h):
        copies = kv_copies(h)

        @pl.when(has_next)
        def _():
            copies[0].start()
            copies[2].start()

        @pl.when(has_prev)
        def _():
            copies[1].start()
            copies[3].start()

    def kv_wait(h):
        copies = kv_copies(h)

        @pl.when(has_prev)
        def _():
            copies[0].wait_recv()
            copies[2].wait_recv()

        @pl.when(has_next)
        def _():
            copies[1].wait_recv()
            copies[3].wait_recv()

    kv_start(0)

    def go_copy(t, left):
        rows = pl.ds(t * TILE, TILE)
        return remote(
            go_ref.at[rows, :], gall.at[rows, aligned(x * COLS, COLS)],
            ga_s.at[left, t], ga_r.at[left, t], x_at(3 if left else 1))

    def go_relay(left):
        at = gall.at[pl.ds(left * TILE, TILE), aligned((x + (1 if left else 3)) % 4 * COLS, COLS)]
        return remote(at, at, gf_s.at[left], gf_r.at[left], x_at(3 if left else 1))

    go_copy(0, 0).start()
    go_copy(1, 1).start()
    go_copy(1, 0).start()
    go_copy(0, 1).start()

    own = pl.ds(TOK, TOK)
    for side, missing in ((0, s == 0), (1, s == 31)):
        @pl.when(missing)
        def _():
            outside = pl.ds(side * 2 * TOK, TOK)
            kw[outside, :] = jnp.zeros((TOK, COLS), BF)
            vw[outside, :] = jnp.zeros((TOK, COLS), BF)
            hr[1 - side] = jnp.zeros((2, TOK, COLS), BF)

    locals_in = [
        pltpu.make_async_copy(k_ref, kw.at[own, :], local_sem.at[1]),
        pltpu.make_async_copy(v_ref, vw.at[own, :], local_sem.at[2]),
        pltpu.make_async_copy(go_ref, gall.at[:, aligned(x * COLS, COLS)], local_sem.at[3]),
    ]
    for copy in locals_in:
        copy.start()
    for copy in locals_in:
        copy.wait()

    def w_rows(z_at, i, half):
        start = (z_at * 2 + core) * PIECE
        if i < 3:
            return pl.ds(pl.multiple_of(start, 32), PIECE)
        return pl.ds(pl.multiple_of(start + half * HALF, 16), HALF)

    def w_right(i):
        at = wt.at[w_rows((z + 8 - i) % 8, i, 0), :]
        return remote(at, at, wr_s.at[i], wr_r.at[i], z_next)

    def w_left(i):
        at = wt.at[w_rows((z + i) % 8, i, 1), :]
        return remote(at, at, wl_s.at[i], wl_r.at[i], z_prev)

    def w_core(i, z_at):
        at = wt.at[slot(z_at, core), :]
        return remote(at, at, wc_s.at[i], wc_r.at[i], partner)

    def w_ring_start():
        @pl.when(same)
        def _():
            w_self_copy().wait()

        for i in range(2):
            from_self = jnp.logical_and(same, ylo == i)

            @pl.when(jnp.logical_not(from_self))
            def _():
                remote(
                    w_ref, wt.at[slot(z, core), pl.ds(i * COLS, COLS)], wy_s.at[0], wy_r.at[i], partner
                ).wait_recv()

        w_right(0).start()
        w_left(0).start()
        w_core(0, z).start()

    def w_ring_step(i):
        w_right(i - 1).wait_recv()
        if i < 4:
            w_right(i).start()
            w_core(i, (z + 8 - i) % 8).start()
        w_left(i - 1).wait_recv()
        if i < 4:
            w_left(i).start()
        w_core(4 + i if i < 4 else 4, (z + i) % 8).start()

    w_ring_start()
    kv_start(1)

    first = s * 2 - 2

    def forward(h, t):
        rows = aligned(t * TILE, TILE)
        query = q_ref[rows, lanes(h)]
        top = jnp.full((1, TILE), -3e38, F32)
        for j in range(5):
            tile_id = first + t + j
            hit = nb_ref[t, 0] == tile_id
            for i in range(1, 5):
                hit = jnp.logical_or(hit, nb_ref[t, i] == tile_id)
            hit = jnp.logical_and(hit, tile_id >= 0)
            bias = jnp.where(hit, 0.0, NEG_FILL)
            key = kw[aligned((t + j) * TILE, TILE), lanes(h)]
            block = dot_nt(key, query) * (SCALE * LOG2E) + bias
            scores[pl.ds(j * TILE, TILE), :] = block
            top = jnp.maximum(top, jnp.max(block, axis=0, keepdims=True))
        total = jnp.zeros((1, TILE), F32)
        u = h * 2 + t
        for j in range(5):
            e = jnp.exp2(scores[pl.ds(j * TILE, TILE), :] - top)
            total = total + jnp.sum(e, axis=0, keepdims=True)
            probs[u, pl.ds(j * TILE, TILE), :] = e.astype(BF)
        turned = dot_tn(
            vw[pl.ds(pl.multiple_of(t * TILE, TILE), WIN), lanes(h)], probs[u]
        )
        inv = 1.0 / total
        inv_total[u] = inv
        att[rows, pl.ds(pl.multiple_of(ylo * COLS + h * HD, HD), HD)] = (turned * inv).T.astype(BF)

    def att_copy(h):
        at = att.at[:, pl.ds(pl.multiple_of(ylo * COLS + h * HD, HD), HD)]
        return remote(at, at, at_s.at[h], at_r.at[h], y_partner)

    def fwd_step(u, carry):
        h, t = u // 2, u % 2

        @pl.when(t == 0)
        def _():
            kv_wait(h)

        @pl.when(u == 1)
        def _():
            kv_start(2)
            w_ring_step(1)

        @pl.when(u == 2)
        def _():
            go_copy(0, 0).wait_recv()
            go_relay(0).start()
            go_copy(1, 1).wait_recv()
            go_relay(1).start()

        for i in range(2, 4):
            @pl.when(u == 2 * i - 1)
            def _():
                w_ring_step(i)

        forward(h, t)

        @pl.when(t == 1)
        def _():
            att_copy(h).start()

        return carry

    lax.fori_loop(0, 2 * HEADS, fwd_step, 0)
    go_copy(1, 0).wait_recv()
    go_copy(0, 1).wait_recv()
    go_relay(0).wait_recv()
    go_relay(1).wait_recv()

    def gw_half(half):
        at = aligned(half * COLS, COLS)

        def gw_step(i, carry):
            part = dot_tn(gall[:, aligned(i * COLS, COLS)], att[:, at])
            gw[pl.ds(i * 4, 4), :, at] = part.reshape(4, PIECE, COLS)
            return carry

        lax.fori_loop(0, 4, gw_step, 0)

    gw_half(ylo)
    w_ring_step(4)
    for i in range(8):
        w_core(i, z).wait_recv()

    def gr_copy(t):
        rows = aligned(t * TILE, TILE)
        return remote(gsend.at[rows, :], grecv.at[rows, :], gr_s.at[t], gr_r.at[t], y_partner)

    def grad_step(t, carry):
        rows = aligned(t * TILE, TILE)
        block = gall[rows, :]
        gsend[rows, :] = dot_nn(block, wt[:, aligned((1 - ylo) * COLS, COLS)]).astype(BF)
        gr_copy(t).start()
        gown[rows, :] = dot_nn(block, wt[:, aligned(ylo * COLS, COLS)])
        return carry

    lax.fori_loop(0, 2, grad_step, 0)
    for h in range(HEADS):
        att_copy(h).wait_recv()
    gw_half(1 - ylo)

    def gw_cast(i, carry):
        cs[i] = gw[i * 2 + 1 - core].astype(BF)
        return carry

    lax.fori_loop(0, 8, gw_cast, 0)
    core_copy = remote(cs, cr, gc_s, gc_r, partner)
    core_copy.start()
    def g_copy(i, left):
        sent, landed = (ls_s, ls_r) if left else (rs_s, rs_r)
        send, recv = (gleft_s, gleft_r) if left else (gright_s, gright_r)
        at = (i, pl.ds(left * HALF, HALF)) if i == 0 else (i,)
        return remote(sent.at[at], landed.at[at], send.at[i], recv.at[i], z_prev if left else z_next)

    def chip_sum(z_at):
        return gw[z_at * 2 + core] + cr[z_at].astype(F32)

    def g_ring_step(i):
        if i == 0:
            core_copy.wait_recv()
        for left in range(2):
            sent, landed = (ls_s, ls_r) if left else (rs_s, rs_r)
            half = pl.ds(left * HALF, HALF)
            if i > 0:
                g_copy(i - 1, left).wait_recv()
            if i < 4:
                mine = chip_sum((z + 4 + i if left else z + 4 - i) % 8)
                if i > 1:
                    mine = mine + landed[i - 1].astype(F32)
                sent[i] = mine.astype(BF)
                if i == 1:
                    sent[1, half] = (mine[left * HALF:(left + 1) * HALF] + landed[0, half].astype(F32)).astype(BF)
                g_copy(i, left).start()

    def out_copy(i):
        return remote(osend.at[i], orecv.at[i], or_s.at[i], or_r.at[i], x_at(1 if i < 3 else 3))

    def out_part(k):
        return dot_nt(att[...], wt[aligned((x + k) % 4 * COLS, COLS), :])

    def out_send(i, part):
        osend[i] = part.astype(BF)
        out_copy(i).start()

    part = out_part(2)
    out_send(0, part[:TILE])
    out_send(3, part[TILE:])
    part = out_part(3)
    out_send(5, part[:TILE])
    held[1] = part[TILE:]
    g_ring_step(0)
    part = out_part(1)
    out_send(2, part[TILE:])
    held[0] = part[:TILE]
    oown[...] = out_part(0)

    def out_relay():
        for i in range(2):
            out_copy(3 * i).wait_recv()
            out_send(3 * i + 1, held[i] + orecv[3 * i].astype(F32))


    def halo_copy(h, i):
        side, rows = ((0, pl.ds(0, TILE)), (0, pl.ds(TILE, TILE)), (1, pl.ds(0, TOK)))[i]
        return remote(
            hs.at[side, :, rows, lanes(h)], hr.at[side, :, rows, lanes(h)], hk_s.at[h, i], hk_r.at[h, i],
            sp_next if side else sp_prev)

    def halo_send(h, i):
        side, first_row, count = ((0, 0, TILE), (0, TILE, TILE), (1, 0, TOK))[i]
        to = pl.ds(first_row, count)
        at = pl.ds(side * 2 * TOK + first_row, count)

        @pl.when(has_next if side else has_prev)
        def _():
            hs[side, 0, to, lanes(h)] = dka[at, lanes(h)].astype(BF)
            hs[side, 1, to, lanes(h)] = dva[at, lanes(h)].astype(BF)
            halo_copy(h, i).start()

    def backward(h, t):
        rows = pl.ds(t * TILE, TILE)
        u = h * 2 + t
        query = q_ref[rows, lanes(h)]
        grad = gatt[rows, lanes(h)]
        made = att[rows, pl.ds(pl.multiple_of(ylo * COLS + h * HD, HD), HD)]
        delta = jnp.sum((grad.astype(F32) * made.astype(F32)).T, axis=0, keepdims=True)
        inv = inv_total[u]
        factor = inv * SCALE
        shift = delta * factor
        inv_rows = jnp.broadcast_to(inv, (HD, TILE)).T
        grad_scaled = (grad.astype(F32) * inv_rows).astype(BF)
        turned = jnp.zeros((HD, TILE), F32)
        for j in ((0, 1, 2, 3, 4), (0, 3, 4, 1, 2))[t]:
            at = pl.ds((t + j) * TILE, TILE)
            key = kw[at, lanes(h)]
            value = vw[at, lanes(h)]
            prob = probs[u, pl.ds(j * TILE, TILE), :]
            inner = dot_nt(value, grad)
            ds = (prob.astype(F32) * (inner * factor - shift)).astype(BF)
            dk = dot_nn(ds, query)
            dv = dot_nn(prob, grad_scaled)
            if t == 0 or j == 4:
                dka[at, lanes(h)] = dk
                dva[at, lanes(h)] = dv
            else:
                dka[at, lanes(h)] += dk
                dva[at, lanes(h)] += dv
            turned = turned + dot_tn(key, ds)
            if t == 0 and j == 0:
                halo_send(h, 0)
            if t == 1 and j == 4:
                halo_send(h, 1)
                halo_send(h, 2)
        gq_ref[rows, lanes(h)] = turned.T.astype(BF)

    def gy_copy(i):
        return remote(ys.at[i], yr.at[yhi], gy_s.at[i], gy_r.at[yhi], device(i, x, ylo, z, core))

    def gy_self():
        return pltpu.make_async_copy(ys.at[ylo], yr.at[yhi], local_sem.at[4])

    def gy_start():
        z_sum = chip_sum(z) + rs_r[3].astype(F32) + ls_r[3].astype(F32)
        ys[0] = z_sum[:, :COLS]
        ys[1] = z_sum[:, COLS:]
        for i in range(2):
            to_self = jnp.logical_and(same, ylo == i)

            @pl.when(jnp.logical_not(to_self))
            def _():
                gy_copy(i).start()

        @pl.when(same)
        def _():
            gy_self().start()

    def grad_ready(t):
        gr_copy(t).wait_recv()
        rows = pl.ds(t * TILE, TILE)
        gatt[rows, :] = (gown[rows, :] + grecv[rows, :].astype(F32)).astype(BF)

    def bwd_step(i, carry):
        h = jnp.where(i < 4, i % 2, 2)
        t = jnp.where(i < 4, i // 2, i - 4)

        @pl.when(i == 0)
        def _():
            grad_ready(0)

        @pl.when(i == 1)
        def _():
            g_ring_step(1)

        @pl.when(i == 2)
        def _():
            grad_ready(1)
            out_relay()
            g_ring_step(2)

        @pl.when(i == 3)
        def _():
            g_ring_step(3)

        @pl.when(t == 0)
        def _():
            backward(h, 0)

        @pl.when(t == 1)
        def _():
            backward(h, 1)

        return carry

    lax.fori_loop(0, 2 * HEADS, bwd_step, 0)

    g_ring_step(4)
    gy_start()

    for i in (1, 2, 4, 5):
        out_copy(i).wait_recv()
    for t, i, j in ((0, 1, 5), (1, 4, 2)):
        rows = pl.ds(t * TILE, TILE)
        out_ref[rows, :] = (oown[rows, :] + orecv[i].astype(F32) + orecv[j].astype(F32)).astype(BF)

    for h in range(HEADS):
        @pl.when(has_next)
        def _():
            halo_copy(h, 0).wait_recv()
            halo_copy(h, 1).wait_recv()

        @pl.when(has_prev)
        def _():
            halo_copy(h, 2).wait_recv()

        at = pl.ds(h * HD, HD)
        gk_ref[:, at] = (
            dka[own, at] + hr[0, 0, :, at].astype(F32) + hr[1, 0, :, at].astype(F32)
        ).astype(BF)
        gv_ref[:, at] = (
            dva[own, at] + hr[0, 1, :, at].astype(F32) + hr[1, 1, :, at].astype(F32)
        ).astype(BF)

    @pl.when(same)
    def _():
        gy_self().wait()

    for i in range(2):
        from_self = jnp.logical_and(same, yhi == i)

        @pl.when(jnp.logical_not(from_self))
        def _():
            remote(ys.at[i], yr.at[i], gy_s.at[i], gy_r.at[i], partner).wait_recv()

    gw_ref[...] = yr[0] + yr[1]

    for k in range(2):
        to_self = jnp.logical_and(same, yhi == k)

        @pl.when(jnp.logical_not(to_self))
        def _():
            w_out_copy(k).wait_send()

    for i in range(2):
        to_self = jnp.logical_and(same, ylo == i)

        @pl.when(jnp.logical_not(to_self))
        def _():
            gy_copy(i).wait_send()

    for h in range(HEADS):
        copies = kv_copies(h)

        @pl.when(has_next)
        def _():
            for copy in (copies[0], copies[2], halo_copy(h, 2)):
                copy.wait_send()

        @pl.when(has_prev)
        def _():
            for copy in (copies[1], copies[3], halo_copy(h, 0), halo_copy(h, 1)):
                copy.wait_send()

        att_copy(h).wait_send()
    for t in range(2):
        gr_copy(t).wait_send()
        go_copy(t, 0).wait_send()
        go_copy(t, 1).wait_send()
        go_relay(t).wait_send()
    for i in range(6):
        out_copy(i).wait_send()
    for i in range(4):
        w_right(i).wait_send()
        w_left(i).wait_send()
        g_copy(i, 0).wait_send()
        g_copy(i, 1).wait_send()
    for i in range(8):
        w_core(i, z).wait_send()
    core_copy.wait_send()


def deliver(*refs):
    for source, target in zip(refs[:5], refs[5:]):
        target[...] = source[...]


def local(queries, keys, values, w_out, grad_out, neighbors):
    vmem = lambda shape, dtype: pltpu.VMEM(shape, dtype)
    dma = lambda *shape: pltpu.SemaphoreType.DMA(shape)
    big = jax.ShapeDtypeStruct((TOK, COLS), BF)
    anywhere = pl.BlockSpec(memory_space=pl.ANY)
    whole = pl.BlockSpec(memory_space=pltpu.VMEM)
    out, gq, gk, gv, gwt = pl.pallas_call(
        kernel,
        out_shape=(big, big, big, big, jax.ShapeDtypeStruct((PIECE, COLS), F32)),
        in_specs=[pl.BlockSpec(memory_space=pltpu.SMEM), whole, anywhere, anywhere, anywhere, anywhere],
        out_specs=[whole] * 5,
        scratch_shapes=[
            vmem((WIDE, COLS), BF), vmem((WIDE, COLS), BF),
            vmem((TOK, 4 * COLS), BF), vmem((4 * COLS, 2 * COLS), BF), vmem((TOK, 2 * COLS), BF),
            vmem((WIN, TILE), F32), vmem((2 * HEADS, WIN, TILE), BF), vmem((2 * HEADS, 1, TILE), F32),
            vmem((TOK, COLS), BF), vmem((TOK, COLS), BF), vmem((TOK, COLS), F32), vmem((TOK, COLS), BF),
            vmem((6, TILE, COLS), BF), vmem((6, TILE, COLS), BF), vmem((TOK, COLS), F32), vmem((2, TILE, COLS), F32),
            vmem((16, PIECE, 2 * COLS), F32),
            vmem((8, PIECE, 2 * COLS), BF), vmem((8, PIECE, 2 * COLS), BF),
            vmem((4, PIECE, 2 * COLS), BF), vmem((4, PIECE, 2 * COLS), BF),
            vmem((4, PIECE, 2 * COLS), BF), vmem((4, PIECE, 2 * COLS), BF),
            vmem((2, PIECE, COLS), F32), vmem((2, PIECE, COLS), F32),
            vmem((WIDE, COLS), F32), vmem((WIDE, COLS), F32),
            vmem((2, 2, TOK, COLS), BF), vmem((2, 2, TOK, COLS), BF),
            dma(5), dma(2), dma(2), dma(4), dma(4), dma(4), dma(4), dma(8), dma(8),
            dma(3, 4), dma(3, 4), dma(2, 2), dma(2, 2), dma(2), dma(2), dma(3), dma(3), dma(2), dma(2), dma(6), dma(6),
            pltpu.SemaphoreType.DMA, pltpu.SemaphoreType.DMA, dma(4), dma(4), dma(4), dma(4), dma(2), dma(2),
            dma(3, 3), dma(3, 3),
        ],
        compiler_params=pltpu.CompilerParams(
            collective_id=0, has_side_effects=True, vmem_limit_bytes=62 * 2**20
        ),
        name="block",
    )(neighbors, queries, keys, values, w_out.T, grad_out)
    out, gq, gk, gv, gwt = pl.pallas_call(
        deliver,
        out_shape=(big, big, big, big, jax.ShapeDtypeStruct((PIECE, COLS), F32)),
        in_specs=[whole] * 5,
        out_specs=[whole] * 5,
        name="deliver",
    )(out, gq, gk, gv, gwt)
    return (out, gq, gk, gv, gwt.T)


def solution(mesh):
    placed = (
        P("sp", "fsdp"),
        P("sp", "fsdp"),
        P("sp", "fsdp"),
        P("fsdp", "sp"),
        P("sp", "fsdp"),
        P("sp", None),
    )
    return jax.shard_map(
        local,
        mesh=mesh,
        in_specs=placed,
        out_specs=(
            P("sp", "fsdp"),
            P("sp", "fsdp"),
            P("sp", "fsdp"),
            P("sp", "fsdp"),
            P("fsdp", "sp"),
        ),
        check_vma=False,
    )
```
